128 devices in a mesh: pool: 16 (over x, z), head: 8 (over y, core).
Axes of the slice: x: 4, y: 4, z: 4, core: 2. Of those that a mesh axis runs over, the one named last changes fastest.
Arguments:
- light_query: bfloat16 [8192, 8192], P('pool', 'head'), may hold values from -6 to 6
- light_key: bfloat16 [8192, 8192], P('pool', 'head'), may hold values from -0.5 to 0.5
- light_value: bfloat16 [8192, 8192], P('pool', 'head'), may hold values from -40 to 40
- light_gate: bfloat16 [8192, 8192], P('pool', 'head'), may hold values from -6 to 6
- decay_rate: float32 [64], P('head'), may hold values from 0.001 to 0.06
- norm_gain: float32 [8192], P('head'), may hold values from 0.5 to 1.5
- state_store: float32 [64, 64, 128, 128], P('pool', 'head'), may hold values from -6 to 6
- state_slot: int32 [64, 64], P('pool', 'head'), may hold values from 0 to 63, as said below
- soft_query: bfloat16 [8192, 8192], P('pool', 'head'), may hold values from -120 to 120
- soft_pair: bfloat16 [8192, 2048], P('pool', 'head'), may hold values from -6 to 6
- kv_store: bfloat16 [2048, 8, 128, 256], P(('pool', 'head')), may hold values from -8 to 8
- page_holder: int32 [64, 32, 1], P('pool'), may hold values from 0 to 127; in each aligned block of 128 rows (0 to 127, 128 to 255, ..., all dimensions but the last counted through in order) at most 2 rows name the same one
- page_local: int32 [64, 32], P('pool'), may hold values from 0 to 15
- prefix_len: int32 [64], P('pool'), may hold values from 1 to 4096, as said below
Outputs:
- light_out: bfloat16 [8192, 8192], P('pool', 'head')
- new_state: float32 [64, 64, 128, 128], P('pool', 'head')
- soft_out: bfloat16 [8192, 8192], P('pool', 'head')
The draws below stay inside these ranges and needn't reach their ends.
Inputs may be any that keep to these rules, and one draw needn't show every extreme that they name: `state_slot`: A slot names holder row slot // 4. In one device's block of 4 requests by 8 heads at most 4 slots lie on one holder row, and every block has a holder row with exactly 4. `page_holder`: devices are numbered pool index times 8 plus head index. `prefix_len`: some request has the full 32 pages of 128 tokens in every draw; page slots past a request's length are not read.
All inputs are finite; a program needn't handle non-finite values.
Results may differ from the reference program's by a relative error of at most 0.0047.
Values may be sent and summed in bfloat16 or wider, within the bound.
A program may use at most 128 MiB of HBM per device.

```python
import math
import jax
import jax.numpy as jnp
import numpy as np
from jax import lax

HEADS = 64
HD = 128
KV_HEADS = 8
SUF = 128
PAGE = 128
MAX_PAGES = 32
REQ_DEV = 4
STATE_DEV = 4
PAGES_DEV = 16
OWNERS = 16
HEAD_GROUPS = 8
HOLDERS = 128
GROUP_HEADS = 8
REQUESTS = 64
TOKENS = 8192
STATE_MOST = 4
PAGE_MOST = 2


def draw_soft_query(key, part):
    key = jax.random.fold_in(key, 11)
    first = jax.random.fold_in(key, 0)
    shape = (TOKENS, HEADS, HD)
    values = jax.random.normal(first, shape, jnp.float32)
    return jnp.clip(values, -120.0, 120.0).reshape(TOKENS, HEADS * HD).astype(jnp.bfloat16)


def draw_kv_store(key, part):
    key = jax.random.fold_in(key, 12)
    first = jax.random.fold_in(key, 0)
    shape = (HOLDERS * PAGES_DEV, KV_HEADS, PAGE, 2 * HD)
    values = jax.random.normal(first, shape, jnp.float32)
    return jnp.clip(values, -8.0, 8.0).astype(jnp.bfloat16)


def draw_light_value(key, part):
    key = jax.random.fold_in(key, 13)
    first, second = jax.random.split(key, 2)
    jitter = jnp.exp(jax.random.uniform(second, (HEADS,), jnp.float32, -0.35, 0.35))
    climb = jnp.arange(HEADS).astype(jnp.float32) / HEADS
    base = jax.random.normal(first, (TOKENS, HEADS, HD), jnp.float32)
    scales = 0.3 * jnp.exp(2.302585 * climb) * jitter
    return jnp.clip(base * scales[None, :, None], -40.0, 40.0).reshape(TOKENS, HEADS * HD).astype(jnp.bfloat16)


def draw_state_slot(key, part):
    key = jax.random.fold_in(key, 14)
    first, second = jax.random.split(key, 2)
    blocks = OWNERS * HEAD_GROUPS
    entries = REQ_DEV * GROUP_HEADS

    def one_block(block_key):
        pieces = jax.random.split(block_key, 3)
        heavy = jax.random.randint(pieces[0], (), 0, OWNERS)
        others = (heavy + 1 + jax.random.permutation(pieces[1], OWNERS - 1)) % OWNERS
        order = jnp.arange(entries)
        listing = jnp.where(order < STATE_MOST, heavy, others[(order - STATE_MOST) % (OWNERS - 1)])
        return jax.random.permutation(pieces[2], listing)
    holder_rows = jax.vmap(one_block)(jax.random.split(first, blocks))
    locals_drawn = jax.random.randint(second, (blocks, entries), 0, STATE_DEV)
    slots = holder_rows * STATE_DEV + locals_drawn
    return slots.reshape(OWNERS, HEAD_GROUPS, REQ_DEV, GROUP_HEADS).transpose(0, 2, 1, 3).reshape(REQUESTS, HEADS).astype(jnp.int32)


def draw_prefix_len(key, part):
    key = jax.random.fold_in(key, 15)
    first, second = jax.random.split(key, 2)
    longest = MAX_PAGES * PAGE
    lengths = jax.random.randint(first, (REQUESTS,), 1, longest + 1)
    chosen = jax.random.randint(second, (), 0, REQUESTS)
    return jnp.where(jnp.arange(REQUESTS) == chosen, longest, lengths).astype(jnp.int32)


def place_ends(values, key, low, top_value):
    longest = values.shape.index(max(values.shape))
    spots = []
    for shift in (0, 1):
        where = [jax.random.randint(jax.random.fold_in(key, axis), (), 0, length) for axis, length in enumerate(values.shape)]
        where[longest] = (where[longest] + shift) % values.shape[longest]
        spots.append(tuple(where))
    return values.at[spots[0]].set(low).at[spots[1]].set(top_value)


def steps_of(stream_key, dims, cuts, least, high):
    gain = 1.0
    for dim, shards_of in cuts:
        heights = jax.random.uniform(jax.random.fold_in(jax.random.fold_in(stream_key, 6), dim), (shards_of,), jnp.float32, least / len(cuts), high / len(cuts))
        gain = gain * jnp.repeat(jnp.exp(heights), dims[dim] // shards_of).reshape((-1,) + (1,) * (len(dims) - 1 - dim))
    return gain


def routed_block(stream_key, own, number, rows, amount, top, most, lean):
    ranking = jax.random.permutation(stream_key, amount)
    crowded, ordinary = shares(amount, rows * top, most, lean, True), shares(amount, rows * top, most, lean, False)
    places = jnp.arange(amount)

    def named(sizes, offset_by):
        used = int((sizes > 0).sum())
        fixed = max(1, used // 4)
        shifted = fixed + (places - fixed + offset_by * (used - fixed)) % max(1, amount - fixed)
        return jnp.zeros((amount,), jnp.int32).at[ranking[jnp.where(places < fixed, places, shifted)]].set(jnp.asarray(sizes, jnp.int32))

    sizes = jnp.where(number % 4 == 0, named(crowded, number // 4), named(ordinary, number - number // 4 - 1))
    mixed = jax.random.permutation(jax.random.fold_in(own, 3), amount)
    giver, taker = mixed[0:amount // 2 * 2:2], mixed[1:amount // 2 * 2:2]
    slack = jnp.minimum(sizes[giver] - 1, most - sizes[taker]) // 2
    slack = jnp.where((giver == ranking[0]) | (taker == ranking[0]) | (sizes[taker] == 0), 0, jnp.maximum(slack, 0))
    shifted = jax.random.randint(jax.random.fold_in(own, 4), (amount // 2,), 0, 1 << 20) % (slack + 1)
    sizes = sizes.at[giver].add(-shifted).at[taker].add(shifted)
    items = jnp.searchsorted(jnp.cumsum(sizes), jnp.arange(rows * top), side="right").astype(jnp.int32)
    table = items.reshape(top, rows).T
    table = table[jax.random.permutation(jax.random.fold_in(own, 1), rows)]
    offset_by = jax.random.randint(jax.random.fold_in(own, 2), (rows, 1), 0, top)
    return jnp.take_along_axis(table, (jnp.arange(top)[None, :] + offset_by) % top, axis=1)


def shares(number_of, total, reach, lean, full):
    portions = [(1 << 20) // math.isqrt(grade ** lean) + 1 for grade in range(1, number_of + 1)]
    largest = reach if full else min(reach, max(-(-total // number_of), total * portions[0] // sum(portions)))
    least = 1 if total - largest >= number_of - 1 else 0
    holding, spare = [largest] + [least] * (number_of - 1), total - largest - least * (number_of - 1)
    while spare > 0:
        free = [i for i in range(1, number_of) if holding[i] < largest] or [i for i in range(1, number_of) if holding[i] < reach]
        whole, remaining = sum([portions[i] for i in free]), spare
        for i in free:
            more = min(reach - holding[i], max(1, remaining * portions[i] // whole), spare)
            holding[i] = holding[i] + more
            spare = spare - more
    return np.array(holding)


def scatter_about(key, dims, width, bound, cuts=(), kind=jnp.bfloat16):
    values = jax.random.normal(key, dims, jnp.float32) * width
    if len(cuts) > 0:
        values = steps_of(key, dims, cuts, -0.22, 0.18) * values
    return jnp.clip(values, min=-bound, max=bound).astype(kind)


def setup_inputs(seed: int = 0) -> dict:
    key_list = jax.random.split(jax.random.key(seed), 15)
    light_query = scatter_about(key_list[0], (TOKENS, HEADS * HD), 1.0, 6.0, ((0, 16), (1, 8)))
    light_key = scatter_about(key_list[1], (TOKENS, HEADS * HD), 0.088, 0.5, ((0, 16), (1, 8)))
    light_value = draw_light_value(jax.random.fold_in(key_list[14], 71), 0)
    light_gate = scatter_about(key_list[3], (TOKENS, HEADS * HD), 1.0, 6.0, ((0, 16), (1, 8)))
    decay_rate = jnp.clip(jnp.exp(math.log(0.06) - 4.0943445 * jax.random.uniform(key_list[4], (HEADS,), jnp.float32) ** steps_of(key_list[4], (HEADS,), ((0, 8),), -0.2, 0.2)), 0.001, 0.06)
    norm_gain = jnp.clip(1.0 + 0.1 * jax.random.normal(key_list[5], (HEADS * HD,), jnp.float32), 0.5, 1.5)
    state_store = scatter_about(key_list[6], (OWNERS * STATE_DEV, HEADS, HD, HD), 1.0, 6.0, ((0, 16), (1, 8)), jnp.float32)
    state_slot = draw_state_slot(jax.random.fold_in(key_list[14], 71), 0)
    soft_query = draw_soft_query(jax.random.fold_in(key_list[14], 71), 0)
    soft_pair = scatter_about(key_list[9], (TOKENS, KV_HEADS * 2 * HD), 1.0, 6.0, ((0, 16), (1, 8)))
    kv_store = draw_kv_store(jax.random.fold_in(key_list[14], 71), 0)
    page_holder_keys = jax.random.split(jax.random.fold_in(key_list[11], 1), REQUESTS * MAX_PAGES // (REQ_DEV * MAX_PAGES))
    page_holder_turns = jax.random.permutation(jax.random.fold_in(key_list[11], 3), REQUESTS * MAX_PAGES // (REQ_DEV * MAX_PAGES))
    page_holder = jax.vmap(lambda own, number: routed_block(jax.random.fold_in(key_list[11], 2), own, number, REQ_DEV * MAX_PAGES, HOLDERS, 1, PAGE_MOST, 2))(page_holder_keys, page_holder_turns).reshape((REQUESTS, MAX_PAGES, 1))
    page_local = place_ends(jax.random.randint(key_list[12], (REQUESTS, MAX_PAGES), 0, PAGES_DEV), jax.random.fold_in(key_list[12], 1), 0, PAGES_DEV - 1).astype(jnp.int32)
    prefix_len = draw_prefix_len(jax.random.fold_in(key_list[14], 71), 0)
    return dict(light_query=light_query, light_key=light_key, light_value=light_value, light_gate=light_gate, decay_rate=decay_rate, norm_gain=norm_gain, state_store=state_store, state_slot=state_slot, soft_query=soft_query, soft_pair=soft_pair, kv_store=kv_store, page_holder=page_holder, page_local=page_local, prefix_len=prefix_len)


def lightning(queries, keys_in, values_in, rates_in, initial):
    length = queries.shape[1]
    highest = lax.Precision.HIGHEST
    query_wide = queries.astype(jnp.float32)
    key_wide = keys_in.astype(jnp.float32)
    value_wide = values_in.astype(jnp.float32)
    offsets = jnp.arange(length).astype(jnp.float32)
    spacing = offsets[:, None] - offsets[None, :]
    weights = jnp.exp(-rates_in[:, None, None] * jnp.maximum(spacing, 0.0)[None]) * (spacing >= 0.0).astype(jnp.float32)[None]
    scores = jnp.einsum('rthd,rshd->rhts', query_wide, key_wide, precision=highest) * weights[None]
    rounded = lax.optimization_barrier(scores.astype(jnp.bfloat16)).astype(jnp.float32)
    inside = jnp.einsum('rhts,rshe->rthe', rounded, value_wide, precision=highest)
    leading = jnp.exp(-rates_in[None, :] * (offsets[:, None] + 1.0))
    carried = jnp.einsum('rthd,rhde->rthe', query_wide * leading[None, :, :, None], initial, precision=highest)
    trailing = jnp.exp(-rates_in[None, :] * (length - 1.0 - offsets[:, None]))
    updated = jnp.exp(-rates_in * length)[None, :, None, None] * initial + jnp.einsum('rshd,rshe->rhde', key_wide * trailing[None, :, :, None], value_wide, precision=highest)
    return (inside + carried, updated)

def attend(query_rows, suffix_kv, prefix_kv, length):
    suffix = query_rows.shape[0]
    key_heads = prefix_kv.shape[1]
    head_width = prefix_kv.shape[-1] // 2
    group_size = query_rows.shape[1] // head_width // key_heads
    grouped = query_rows.reshape(suffix, key_heads, group_size, head_width).transpose(1, 2, 0, 3).reshape(key_heads, group_size * suffix, head_width)
    earlier = prefix_kv.transpose(1, 0, 2, 3).reshape(key_heads, -1, 2 * head_width)
    recent = suffix_kv.reshape(suffix, key_heads, 2 * head_width).transpose(1, 0, 2)
    joined = jnp.concatenate([earlier, recent], axis=1)
    cached_count = earlier.shape[1]
    column = jnp.arange(cached_count + suffix)
    moment = jnp.arange(group_size * suffix) % suffix
    allowed = jnp.where(column[None, :] < cached_count, column[None, :] < length, column[None, :] - cached_count <= moment[:, None])
    temper = 1.0 / math.sqrt(head_width)

    def per_head(operands):
        group_query, group_pair = operands
        scores = jnp.dot(group_query, group_pair[:, :head_width].T, preferred_element_type=jnp.float32) * temper
        scores = jnp.where(allowed, scores, -1e+30)
        highest = lax.optimization_barrier(jnp.max(scores, axis=1, keepdims=True))
        lifted = jnp.exp(scores - highest)
        totals = lax.optimization_barrier(jnp.sum(lifted, axis=1, keepdims=True))
        mixed = jnp.dot(lifted.astype(jnp.bfloat16), group_pair[:, head_width:], preferred_element_type=jnp.float32)
        return mixed / totals
    result = lax.map(per_head, (grouped, joined))
    return result.reshape(key_heads, group_size, suffix, head_width).transpose(2, 0, 1, 3).reshape(suffix, key_heads * group_size * head_width).astype(jnp.bfloat16)

def reference(light_query, light_key, light_value, light_gate, decay_rate, norm_gain, state_store, state_slot, soft_query, soft_pair, kv_store, page_holder, page_local, prefix_len):

    def one_request(position):
        first_row = position * SUF

        def rows_of(array):
            return lax.dynamic_slice_in_dim(array, first_row, SUF, 0)
        query_block = rows_of(light_query).reshape(1, SUF, HEADS, HD)
        key_block = rows_of(light_key).reshape(1, SUF, HEADS, HD)
        value_block = rows_of(light_value).reshape(1, SUF, HEADS, HD)
        initial = state_store[state_slot[position], jnp.arange(HEADS)]
        output, updated = lightning(query_block, key_block, value_block, decay_rate, initial[None])
        squares = lax.optimization_barrier(jnp.sum(output * output, axis=(2, 3))).reshape(SUF, 1)
        factor = lax.rsqrt(squares / (HEADS * HD) + 1e-06)
        normed = output.reshape(SUF, HEADS * HD) * factor * norm_gain * jax.nn.sigmoid(rows_of(light_gate).astype(jnp.float32))
        pages = page_holder[position, :, 0] * PAGES_DEV + page_local[position]
        prefix = kv_store[pages]
        soft = attend(rows_of(soft_query), rows_of(soft_pair), prefix, prefix_len[position])
        return (normed.astype(jnp.bfloat16), updated[0], soft)
    light, states, soft = lax.map(one_request, jnp.arange(REQUESTS, dtype=jnp.int32))
    return (light.reshape(TOKENS, HEADS * HD), states, soft.reshape(TOKENS, HEADS * HD))
```

```python
import functools
import math

import jax
import jax.numpy as jnp
from jax import lax
from jax.experimental import pallas as pl
from jax.experimental.pallas import tpu as pltpu
from jax.sharding import PartitionSpec as P


def lightning(queries, keys_in, values_in, rates_in, initial):
    length = queries.shape[1]
    highest = lax.Precision.HIGHEST
    offsets = jnp.arange(length).astype(jnp.float32)
    spacing = offsets[:, None] - offsets[None, :]
    weights = (
        jnp.exp(-rates_in[:, None, None] * jnp.maximum(spacing, 0.0)[None])
        * (spacing >= 0.0).astype(jnp.float32)[None]
    )
    scores = (
        jnp.einsum("rthd,rshd->rhts", queries, keys_in, preferred_element_type=jnp.float32)
        * weights[None]
    )
    rounded = scores.astype(jnp.bfloat16)
    inside = jnp.einsum("rhts,rshe->rthe", rounded, values_in, preferred_element_type=jnp.float32)
    leading = jnp.exp(-rates_in[None, :] * (offsets[:, None] + 1.0))
    carried = jnp.einsum(
        "rthd,rhde->rthe",
        queries.astype(jnp.float32) * leading[None, :, :, None],
        initial,
        precision=highest,
    )
    trailing = jnp.exp(-rates_in[None, :] * (length - 1.0 - offsets[:, None]))
    updated = jnp.exp(-rates_in * length)[None, :, None, None] * initial + jnp.einsum(
        "rshd,rshe->rhde",
        keys_in.astype(jnp.float32) * trailing[None, :, :, None],
        values_in.astype(jnp.float32),
        precision=highest,
    )
    return (inside + carried, updated)


def attend(query_rows, suffix_kv, prefix_kv, length):
    suffix = query_rows.shape[0]
    key_heads = prefix_kv.shape[1]
    head_width = prefix_kv.shape[-1] // 2
    group_size = query_rows.shape[1] // head_width // key_heads
    grouped = (
        query_rows.reshape(suffix, key_heads, group_size, head_width)
        .transpose(1, 2, 0, 3)
        .reshape(key_heads, group_size * suffix, head_width)
    )
    earlier = prefix_kv.transpose(1, 0, 2, 3).reshape(key_heads, -1, 2 * head_width)
    recent = suffix_kv.reshape(suffix, key_heads, 2 * head_width).transpose(1, 0, 2)
    joined = jnp.concatenate([earlier, recent], axis=1)
    cached_count = earlier.shape[1]
    column = jnp.arange(cached_count + suffix)
    moment = jnp.arange(group_size * suffix) % suffix
    allowed = jnp.where(
        column[None, :] < cached_count,
        column[None, :] < length,
        column[None, :] - cached_count <= moment[:, None],
    )
    temper = 1.0 / math.sqrt(head_width)

    def per_head(operands):
        group_query, group_pair = operands
        scores = (
            jnp.dot(group_query, group_pair[:, :head_width].T, preferred_element_type=jnp.float32)
            * temper
        )
        scores = jnp.where(allowed, scores, -1e30)
        highest = jnp.max(scores, axis=1, keepdims=True)
        lifted = jnp.exp(scores - highest)
        totals = jnp.sum(lifted, axis=1, keepdims=True)
        mixed = jnp.dot(
            lifted.astype(jnp.bfloat16),
            group_pair[:, head_width:],
            preferred_element_type=jnp.float32,
        )
        return mixed / totals

    result = lax.map(per_head, (grouped, joined))
    return (
        result.reshape(key_heads, group_size, suffix, head_width)
        .transpose(2, 0, 1, 3)
        .reshape(suffix, key_heads * group_size * head_width)
        .astype(jnp.bfloat16)
    )


def plan_lists(holder_ids, local_ids, holder_count, capacity):
    matches = (holder_ids[:, None] == jnp.arange(holder_count, dtype=jnp.int32)[None, :]).astype(
        jnp.int32
    )
    before = jnp.cumsum(matches, axis=0) - matches
    ranking = jnp.sum(before * matches, axis=1)
    chosen = matches.T[:, None, :] * (
        ranking[None, None, :] == jnp.arange(capacity, dtype=jnp.int32)[None, :, None]
    ).astype(jnp.int32)
    requests_out = jnp.sum(chosen * local_ids[None, None, :], axis=2)
    return (requests_out, holder_ids * capacity + ranking)


def state_entries(slot_rows, stored_states, group_heads):
    flat_slots = slot_rows.reshape(-1)
    within = jnp.tile(jnp.arange(group_heads, dtype=jnp.int32), flat_slots.shape[0] // group_heads)
    return (flat_slots // stored_states, flat_slots % stored_states * group_heads + within)


def general_body(
    light_query,
    light_key,
    light_value,
    light_gate,
    decay_rate,
    norm_gain,
    state_store,
    state_slot,
    soft_query,
    soft_pair,
    kv_store,
    page_holder,
    page_local,
    prefix_len,
):
    owners = lax.axis_size("pool")
    groups = lax.axis_size("head")
    holders = owners * groups
    requests = prefix_len.shape[0]
    group_heads = decay_rate.shape[0]
    head_width = state_store.shape[-1]
    stored_states = state_store.shape[0]
    stored_pages = kv_store.shape[0]
    key_heads = kv_store.shape[1] // groups
    page_tokens = kv_store.shape[2]
    max_pages = page_local.shape[1]
    suffix = light_query.shape[0] // requests
    state_capacity = max(2, 2 * requests * group_heads // owners)
    page_capacity = max(2, 2 * requests * max_pages // holders)
    state_holders, state_locals = state_entries(state_slot, stored_states, group_heads)
    state_asks, state_picks = plan_lists(state_holders, state_locals, owners, state_capacity)
    page_asks, page_picks = plan_lists(
        page_holder.reshape(-1), page_local.reshape(-1), holders, page_capacity
    )
    state_served = lax.all_to_all(state_asks, "pool", split_axis=0, concat_axis=0, tiled=True)
    page_served = lax.all_to_all(
        page_asks, ("pool", "head"), split_axis=0, concat_axis=0, tiled=True
    )
    flat_states = state_store.reshape(stored_states * group_heads, head_width, head_width)
    outgoing = jnp.take(flat_states, state_served.reshape(-1), axis=0).reshape(
        owners, state_capacity, head_width, head_width
    )
    arrived = lax.all_to_all(outgoing, "pool", split_axis=0, concat_axis=0, tiled=True)
    initial = jnp.take(
        arrived.reshape(owners * state_capacity, head_width, head_width), state_picks, axis=0
    ).reshape(requests, group_heads, head_width, head_width)
    page_rows = kv_store.reshape(stored_pages * groups, key_heads, page_tokens, 2 * head_width)
    target_head = jnp.arange(holders, dtype=jnp.int32) % groups
    wanted = page_served * groups + target_head[:, None]
    outgoing_pages = jnp.take(page_rows, wanted.reshape(-1), axis=0).reshape(
        holders, page_capacity, key_heads, page_tokens, 2 * head_width
    )
    arrived_pages = lax.all_to_all(
        outgoing_pages, ("pool", "head"), split_axis=0, concat_axis=0, tiled=True
    )
    prefix = jnp.take(
        arrived_pages.reshape(holders * page_capacity, key_heads, page_tokens, 2 * head_width),
        page_picks,
        axis=0,
    ).reshape(requests, max_pages, key_heads, page_tokens, 2 * head_width)
    output, updated = lightning(
        light_query.reshape(requests, suffix, group_heads, head_width),
        light_key.reshape(requests, suffix, group_heads, head_width),
        light_value.reshape(requests, suffix, group_heads, head_width),
        decay_rate,
        initial,
    )
    squares = jnp.sum(output * output, axis=(2, 3))
    totals = lax.psum(squares, "head")
    factor = lax.rsqrt(totals / (groups * group_heads * head_width) + 1e-06)
    normed = (
        output.reshape(requests * suffix, group_heads * head_width)
        * factor.reshape(-1, 1)
        * norm_gain
        * jax.nn.sigmoid(light_gate.astype(jnp.float32))
    )
    light_out = normed.astype(jnp.bfloat16)

    def one_request(position):
        first_row = position * suffix
        return attend(
            lax.dynamic_slice_in_dim(soft_query, first_row, suffix, 0),
            lax.dynamic_slice_in_dim(soft_pair, first_row, suffix, 0),
            prefix[position],
            prefix_len[position],
        )

    soft_out = lax.map(one_request, jnp.arange(requests, dtype=jnp.int32)).reshape(
        requests * suffix, group_heads * head_width
    )
    return (light_out, updated, soft_out)


MESH = pl.DeviceIdType.MESH
LANES = 128
CHUNKS = 8
ROW_CAP = 11
STATE_CAP = 4
LOG2E = 1.4426950408889634


def wait_bytes(ref, sem):
    pltpu.make_async_copy(ref, ref, sem).wait()


def fused_kernel(
    row_cap,
    table,
    rates,
    q_in,
    k_in,
    v_in,
    gate_in,
    gain_in,
    store_in,
    soft_q,
    pair_in,
    kv_ref,
    light_out,
    state_out,
    soft_out,
    a_buf,
    a_cur,
    s_buf,
    r_buf,
    r_cur,
    key_buf,
    val_buf,
    st_send,
    st_recv,
    mix,
    sq_send,
    sq_recv,
    q_cat,
    acc,
    top,
    a_send,
    a_recv,
    b_send,
    b_recv,
    keep_sems,
    st_sems,
    sq_sems,
):
    f32, bf16 = jnp.float32, jnp.bfloat16
    tokens = LANES // CHUNKS
    keys = 32 * tokens
    pool, head = lax.axis_index("pool"), lax.axis_index("head")
    px, pz = pool // 4, lax.rem(pool, 4)
    hy, hc = head // 2, lax.rem(head, 2)
    heads_to = [lax.rem(hy + k // 2, 4) * 2 + lax.rem(hc + k % 2, 2) for k in range(1, 8)]
    pools_to = [lax.rem(px + k // 4, 4) * 4 + lax.rem(pz + k % 4, 4) for k in range(1, 16)]
    pick_at, place_at, len_at = 0, 16 * row_cap, 16 * row_cap + 128
    st_pick_at, st_place_at = len_at + 4, len_at + 4 + 64

    barrier = pltpu.get_barrier_semaphore()
    for d in heads_to:
        pl.semaphore_signal(barrier, inc=1, device_id={"head": d}, device_id_type=MESH)
    for d in pools_to:
        pl.semaphore_signal(barrier, inc=1, device_id={"pool": d}, device_id_type=MESH)
    pl.semaphore_wait(barrier, 22)

    def send_store(t, carry):
        part = pl.ds(pl.multiple_of(t * tokens, tokens), tokens)
        for d in heads_to:
            pltpu.make_async_remote_copy(
                kv_ref.at[:, d, part, :],
                a_buf.at[t, pl.ds(head * 16, 16)],
                a_send.at[t],
                a_recv.at[t],
                device_id={"head": d},
                device_id_type=MESH,
            ).start()
        pltpu.make_async_copy(
            kv_ref.at[:, head, part, :], a_buf.at[t, pl.ds(head * 16, 16)], a_recv.at[t]
        ).start()
        return carry

    lax.fori_loop(0, CHUNKS, send_store, 0)

    def pack_state(i, carry):
        for c in range(STATE_CAP):
            st_send[i * STATE_CAP + c] = store_in[table[st_pick_at + i * STATE_CAP + c]].astype(bf16)
        return carry

    lax.fori_loop(0, 16, pack_state, 0)
    mine_st = pl.ds(pool * STATE_CAP, STATE_CAP)
    for d in pools_to:
        pltpu.make_async_remote_copy(
            st_send.at[pl.ds(d * STATE_CAP, STATE_CAP)],
            st_recv.at[mine_st],
            st_sems.at[0],
            st_sems.at[1],
            device_id={"pool": d},
            device_id_type=MESH,
        ).start()
    pltpu.make_async_copy(st_send.at[mine_st], st_recv.at[mine_st], st_sems.at[1]).start()

    temper = LOG2E / math.sqrt(LANES)
    val_buf[:, LANES:] = jnp.ones((keys, LANES), bf16)
    row_i = lax.broadcasted_iota(jnp.int32, (LANES, LANES), 0)
    col_i = lax.broadcasted_iota(jnp.int32, (LANES, LANES), 1)

    def rows_of(r):
        return pl.ds(pl.multiple_of(r * LANES, LANES), LANES)

    def open_softmax(e, carry):
        r, h = e // 8, lax.rem(e, 8)
        q = soft_q[rows_of(r), rows_of(h)]
        q_cat[r, rows_of(h), :] = q
        k = pair_in[rows_of(r), :LANES]
        v = pair_in[rows_of(r), LANES:]
        s = lax.dot_general(q, k, (((1,), (1,)), ((), ())), preferred_element_type=f32) * temper
        s = jnp.where(col_i <= row_i, s, -1e30)
        peak = jnp.max(s, axis=1, keepdims=True)
        p = jnp.exp2(s - peak).astype(bf16)
        acc[r, rows_of(h), :LANES] = jnp.dot(p, v, preferred_element_type=f32)
        acc[r, rows_of(h), LANES:] = jnp.dot(p, jnp.ones((LANES, LANES), bf16), preferred_element_type=f32)
        top[r, rows_of(h), :] = jnp.broadcast_to(peak, (LANES, LANES))
        return carry

    lax.fori_loop(0, 32, open_softmax, 0)

    lane = lax.broadcasted_iota(jnp.int32, (1, keys), 1)

    def attend_chunk(t):
        wait_bytes(r_buf.at[t, pl.ds(0, 15 * row_cap)], b_recv.at[t])
        r_cur[...] = r_buf[t]
        spot = (lane // tokens) * LANES + t * tokens + lax.rem(lane, tokens)

        def one_request(r, carry):
            for p in range(32):
                block = r_cur[table[place_at + r * 32 + p]]
                key_buf[p * tokens : (p + 1) * tokens, :] = block[:, :LANES]
                val_buf[p * tokens : (p + 1) * tokens, :LANES] = block[:, LANES:]
            bias = jnp.where(spot < table[len_at + r], 0.0, -1e30).astype(f32)

            def one_block(b, inner):
                rows = pl.ds(pl.multiple_of(b * 256, 256), 256)
                s = lax.dot_general(
                    q_cat[r, rows, :], key_buf[...], (((1,), (1,)), ((), ())), preferred_element_type=f32
                )
                s = s * temper + bias
                before = top[r, rows, :1]
                peak = jnp.maximum(before, jnp.max(s, axis=1, keepdims=True))
                p = jnp.exp2(s - peak).astype(bf16)
                acc[r, rows, :] = acc[r, rows, :] * jnp.exp2(before - peak) + jnp.dot(
                    p, val_buf[...], preferred_element_type=f32
                )
                top[r, rows, :] = jnp.broadcast_to(peak, (256, LANES))
                return inner

            return lax.fori_loop(0, 4, one_block, carry)

        lax.fori_loop(0, 4, one_request, 0)

    def light_request(r):
        spacing = (row_i - col_i).astype(f32)
        steps = lax.broadcasted_iota(jnp.int32, (LANES, 1), 0).astype(f32)

        def one_head(h, total):
            rate = rates[h]
            rows, cols = rows_of(r), rows_of(h)
            q, k, v = q_in[rows, cols], k_in[rows, cols], v_in[rows, cols]
            state = st_recv[table[st_place_at + r * 8 + h]]
            weights = jnp.where(spacing >= 0.0, jnp.exp(-rate * jnp.maximum(spacing, 0.0)), 0.0)
            s = lax.dot_general(q, k, (((1,), (1,)), ((), ())), preferred_element_type=f32) * weights
            inside = jnp.dot(s.astype(bf16), v, preferred_element_type=f32)
            carried = jnp.dot(q, state, preferred_element_type=f32) * jnp.exp(-rate * (steps + 1.0))
            out = inside + carried
            mix[rows, cols] = out
            trail = k.astype(f32) * jnp.exp(-rate * (LANES - 1.0 - steps))
            high = trail.astype(bf16)
            low = (trail - high.astype(f32)).astype(bf16)
            across = (((0,), (0,)), ((), ()))
            state_out[r * 8 + h] = (
                state.astype(f32) * jnp.exp(jnp.full((1, 1), -LANES, f32) * rate)
                + lax.dot_general(high, v, across, preferred_element_type=f32)
                + lax.dot_general(low, v, across, preferred_element_type=f32)
            )
            return total + jnp.sum(out * out, axis=1, keepdims=True)

        total = lax.fori_loop(0, 8, one_head, jnp.zeros((LANES, 1), f32))
        sq_send[r] = jnp.broadcast_to(total, (LANES, LANES)).T[:8, :]

    def step(t, carry):
        wait_bytes(a_buf.at[t], a_recv.at[t])
        slot = lax.rem(t, 2)

        @pl.when(t >= 2)
        def _():
            wait_bytes(s_buf.at[slot, pl.ds(0, 15 * row_cap)], b_send.at[slot])
            wait_bytes(s_buf.at[slot, pl.ds(0, row_cap)], keep_sems.at[slot])

        a_cur[...] = a_buf[t]

        def pack(i, inner):
            for c in range(row_cap):
                s_buf[slot, i * row_cap + c] = a_cur[table[pick_at + i * row_cap + c]]
            return inner

        lax.fori_loop(0, 16, pack, 0)
        mine = pl.ds(pool * row_cap, row_cap)
        for d in pools_to:
            pltpu.make_async_remote_copy(
                s_buf.at[slot, pl.ds(d * row_cap, row_cap)],
                r_buf.at[t, mine],
                b_send.at[slot],
                b_recv.at[t],
                device_id={"pool": d},
                device_id_type=MESH,
            ).start()
        pltpu.make_async_copy(s_buf.at[slot, mine], r_buf.at[t, mine], keep_sems.at[slot]).start()

        @pl.when(t == 2)
        def _():
            wait_bytes(st_recv, st_sems.at[1])

        @pl.when((t >= 2) & (t < 6))
        def _():
            light_request(t - 2)

        @pl.when(t == 6)
        def _():
            sq_recv[head] = sq_send[...]
            for d in heads_to:
                pltpu.make_async_remote_copy(
                    sq_send,
                    sq_recv.at[head],
                    sq_sems.at[0],
                    sq_sems.at[1],
                    device_id={"head": d},
                    device_id_type=MESH,
                ).start()

        @pl.when(t >= 2)
        def _():
            attend_chunk(t - 2)

        return carry

    lax.fori_loop(0, CHUNKS, step, 0)
    for slot in range(2):
        wait_bytes(s_buf.at[slot, pl.ds(0, 15 * row_cap)], b_send.at[slot])
        wait_bytes(s_buf.at[slot, pl.ds(0, row_cap)], keep_sems.at[slot])
    wait_bytes(sq_recv.at[pl.ds(0, 7)], sq_sems.at[1])

    def finish_light(r, carry):
        squares = jnp.sum(sq_recv[:, r, :1, :], axis=0)
        factor = lax.rsqrt(squares / (64.0 * LANES) + 1e-06)
        column = jnp.broadcast_to(factor, (LANES, LANES)).T[:, :1]
        rows = rows_of(r)
        gate = jax.nn.sigmoid(gate_in[rows, :].astype(f32))
        light_out[rows, :] = (mix[rows, :] * column * gain_in[...] * gate).astype(bf16)
        return carry

    lax.fori_loop(0, 4, finish_light, 0)
    attend_chunk(CHUNKS - 2)
    attend_chunk(CHUNKS - 1)

    def finish_soft(e, carry):
        r, h = e // 8, lax.rem(e, 8)
        soft_out[rows_of(r), rows_of(h)] = (
            acc[r, rows_of(h), :LANES] / acc[r, rows_of(h), LANES:]
        ).astype(bf16)
        return carry

    lax.fori_loop(0, 32, finish_soft, 0)

    def drain(t, carry):
        wait_bytes(a_buf.at[t, pl.ds(0, 112)], a_send.at[t])
        return carry

    lax.fori_loop(0, CHUNKS, drain, 0)
    wait_bytes(st_send.at[pl.ds(0, 15 * STATE_CAP)], st_sems.at[0])
    wait_bytes(sq_recv.at[pl.ds(0, 7)], sq_sems.at[0])


def fused_call(row_cap, table, rates, q, k, v, gate, gain, store, soft_q, pair, kv):
    tokens = LANES // CHUNKS
    bf16, f32 = jnp.bfloat16, jnp.float32
    vmem, smem = pl.BlockSpec(memory_space=pltpu.VMEM), pl.BlockSpec(memory_space=pltpu.SMEM)
    dma = pltpu.SemaphoreType.DMA
    return pl.pallas_call(
        functools.partial(fused_kernel, row_cap),
        out_shape=(
            jax.ShapeDtypeStruct((512, 1024), bf16),
            jax.ShapeDtypeStruct((32, LANES, LANES), f32),
            jax.ShapeDtypeStruct((512, 1024), bf16),
        ),
        in_specs=[smem, smem] + [vmem] * 8 + [pl.BlockSpec(memory_space=pl.ANY)],
        out_specs=(vmem, vmem, vmem),
        scratch_shapes=[
            pltpu.VMEM((CHUNKS, 128, tokens, 256), bf16),
            pltpu.VMEM((128, tokens, 256), bf16),
            pltpu.VMEM((2, 16 * row_cap, tokens, 256), bf16),
            pltpu.VMEM((CHUNKS, 16 * row_cap, tokens, 256), bf16),
            pltpu.VMEM((16 * row_cap, tokens, 256), bf16),
            pltpu.VMEM((32 * tokens, LANES), bf16),
            pltpu.VMEM((32 * tokens, 2 * LANES), bf16),
            pltpu.VMEM((16 * STATE_CAP, LANES, LANES), bf16),
            pltpu.VMEM((16 * STATE_CAP, LANES, LANES), bf16),
            pltpu.VMEM((512, 1024), f32),
            pltpu.VMEM((4, 8, LANES), f32),
            pltpu.VMEM((8, 4, 8, LANES), f32),
            pltpu.VMEM((4, 1024, LANES), bf16),
            pltpu.VMEM((4, 1024, 2 * LANES), f32),
            pltpu.VMEM((4, 1024, LANES), f32),
            dma((CHUNKS,)),
            dma((CHUNKS,)),
            dma((2,)),
            dma((CHUNKS,)),
            dma((2,)),
            dma((2,)),
            dma((2,)),
        ],
        compiler_params=pltpu.CompilerParams(
            collective_id=1, has_side_effects=True, vmem_limit_bytes=60 * 2**20
        ),
        cost_estimate=pl.CostEstimate(flops=10**10, bytes_accessed=3 * 10**7, transcendentals=2 * 10**7),
    )(table, rates, q, k, v, gate, gain, store, soft_q, pair, kv)


def exclusive_rank(match):
    size = match.shape[-1]
    order = jnp.arange(size)
    before = (order[:, None] < order[None, :]).astype(jnp.bfloat16)
    return jnp.dot(match.astype(jnp.bfloat16), before, preferred_element_type=jnp.float32).astype(jnp.int32)


def pick_lists(match, values, capacity):
    rank = exclusive_rank(match)
    chosen = match[:, None, :] & (rank[:, None, :] == jnp.arange(capacity)[None, :, None])
    return jnp.sum(jnp.where(chosen, values[:, None, :], 0), axis=2).reshape(-1)


def own_places(rows, valid, capacity):
    order = jnp.arange(rows.shape[0])
    same = (rows[:, None] == rows[None, :]) & valid[None, :] & (order[None, :] < order[:, None])
    return rows * capacity + jnp.sum(same.astype(jnp.int32), axis=1)


def plan(state_slot, page_holder, page_local, prefix_len):
    owner = lax.axis_index("pool")
    pages = page_holder[:, :, 0] * 16 + page_local
    active = jnp.arange(32)[None, :] * LANES < prefix_len[:, None]
    own_pages = jnp.where(active, pages, 4095).reshape(-1)
    own_states = state_slot.reshape(-1)
    everyone = lax.all_gather(jnp.concatenate([own_pages, own_states]), "pool")
    all_pages, all_states = everyone[:, :128], everyone[:, 128:]
    page_rows = all_pages // 128
    picks = pick_lists(page_rows == owner, all_pages % 128, ROW_CAP)
    counts = jnp.sum((page_rows[:, :, None] == jnp.arange(16)[None, None, :]).astype(jnp.int32), axis=1)
    fits = jnp.max(counts) <= ROW_CAP
    places = own_places(own_pages // 128, active.reshape(-1), ROW_CAP).reshape(4, 32)
    places = jnp.where(active, places, places[:, :1]).reshape(-1)
    within = jnp.arange(32) % 8
    state_picks = pick_lists(all_states // 4 == owner, all_states % 4 * 8 + within[None, :], STATE_CAP)
    state_places = own_places(own_states // 4, jnp.ones((32,), bool), STATE_CAP)
    table = jnp.concatenate([picks, places, prefix_len, state_picks, state_places]).astype(jnp.int32)
    return table, fits


def body(
    light_query,
    light_key,
    light_value,
    light_gate,
    decay_rate,
    norm_gain,
    state_store,
    state_slot,
    soft_query,
    soft_pair,
    kv_store,
    page_holder,
    page_local,
    prefix_len,
):
    table, fits = plan(state_slot, page_holder, page_local, prefix_len)

    def quick():
        light, states, soft = fused_call(
            ROW_CAP,
            table,
            decay_rate,
            light_query,
            light_key,
            light_value,
            light_gate,
            norm_gain.reshape(1, -1),
            state_store.reshape(32, LANES, LANES),
            soft_query,
            soft_pair,
            kv_store,
        )
        return light, states.reshape(4, 8, LANES, LANES), soft

    def general():
        return general_body(
            light_query,
            light_key,
            light_value,
            light_gate,
            decay_rate,
            norm_gain,
            state_store,
            state_slot,
            soft_query,
            soft_pair,
            kv_store,
            page_holder,
            page_local,
            prefix_len,
        )

    return lax.cond(fits, quick, general)


def solution(mesh):
    return jax.shard_map(
        body,
        mesh=mesh,
        in_specs=(
            P("pool", "head"),
            P("pool", "head"),
            P("pool", "head"),
            P("pool", "head"),
            P("head"),
            P("head"),
            P("pool", "head", None, None),
            P("pool", "head"),
            P("pool", "head"),
            P("pool", "head"),
            P(("pool", "head"), None, None, None),
            P("pool", None, None),
            P("pool", None),
            P("pool"),
        ),
        out_specs=(P("pool", "head"), P("pool", "head", None, None), P("pool", "head")),
        check_vma=False,
    )
```

```python
import functools
import math

import jax
import jax.numpy as jnp
from jax import lax
from jax.experimental import pallas as pl
from jax.experimental.pallas import tpu as pltpu
from jax.sharding import PartitionSpec as P


def lightning(queries, keys_in, values_in, rates_in, initial):
    length = queries.shape[1]
    highest = lax.Precision.HIGHEST
    offsets = jnp.arange(length).astype(jnp.float32)
    spacing = offsets[:, None] - offsets[None, :]
    weights = (
        jnp.exp(-rates_in[:, None, None] * jnp.maximum(spacing, 0.0)[None])
        * (spacing >= 0.0).astype(jnp.float32)[None]
    )
    scores = (
        jnp.einsum("rthd,rshd->rhts", queries, keys_in, preferred_element_type=jnp.float32)
        * weights[None]
    )
    rounded = scores.astype(jnp.bfloat16)
    inside = jnp.einsum("rhts,rshe->rthe", rounded, values_in, preferred_element_type=jnp.float32)
    leading = jnp.exp(-rates_in[None, :] * (offsets[:, None] + 1.0))
    carried = jnp.einsum(
        "rthd,rhde->rthe",
        queries.astype(jnp.float32) * leading[None, :, :, None],
        initial,
        precision=highest,
    )
    trailing = jnp.exp(-rates_in[None, :] * (length - 1.0 - offsets[:, None]))
    updated = jnp.exp(-rates_in * length)[None, :, None, None] * initial + jnp.einsum(
        "rshd,rshe->rhde",
        keys_in.astype(jnp.float32) * trailing[None, :, :, None],
        values_in.astype(jnp.float32),
        precision=highest,
    )
    return (inside + carried, updated)


def attend(query_rows, suffix_kv, prefix_kv, length):
    suffix = query_rows.shape[0]
    key_heads = prefix_kv.shape[1]
    head_width = prefix_kv.shape[-1] // 2
    group_size = query_rows.shape[1] // head_width // key_heads
    grouped = (
        query_rows.reshape(suffix, key_heads, group_size, head_width)
        .transpose(1, 2, 0, 3)
        .reshape(key_heads, group_size * suffix, head_width)
    )
    earlier = prefix_kv.transpose(1, 0, 2, 3).reshape(key_heads, -1, 2 * head_width)
    recent = suffix_kv.reshape(suffix, key_heads, 2 * head_width).transpose(1, 0, 2)
    joined = jnp.concatenate([earlier, recent], axis=1)
    cached_count = earlier.shape[1]
    column = jnp.arange(cached_count + suffix)
    moment = jnp.arange(group_size * suffix) % suffix
    allowed = jnp.where(
        column[None, :] < cached_count,
        column[None, :] < length,
        column[None, :] - cached_count <= moment[:, None],
    )
    temper = 1.0 / math.sqrt(head_width)

    def per_head(operands):
        group_query, group_pair = operands
        scores = (
            jnp.dot(group_query, group_pair[:, :head_width].T, preferred_element_type=jnp.float32)
            * temper
        )
        scores = jnp.where(allowed, scores, -1e30)
        highest = jnp.max(scores, axis=1, keepdims=True)
        lifted = jnp.exp(scores - highest)
        totals = jnp.sum(lifted, axis=1, keepdims=True)
        mixed = jnp.dot(
            lifted.astype(jnp.bfloat16),
            group_pair[:, head_width:],
            preferred_element_type=jnp.float32,
        )
        return mixed / totals

    result = lax.map(per_head, (grouped, joined))
    return (
        result.reshape(key_heads, group_size, suffix, head_width)
        .transpose(2, 0, 1, 3)
        .reshape(suffix, key_heads * group_size * head_width)
        .astype(jnp.bfloat16)
    )


def plan_lists(holder_ids, local_ids, holder_count, capacity):
    matches = (holder_ids[:, None] == jnp.arange(holder_count, dtype=jnp.int32)[None, :]).astype(
        jnp.int32
    )
    before = jnp.cumsum(matches, axis=0) - matches
    ranking = jnp.sum(before * matches, axis=1)
    chosen = matches.T[:, None, :] * (
        ranking[None, None, :] == jnp.arange(capacity, dtype=jnp.int32)[None, :, None]
    ).astype(jnp.int32)
    requests_out = jnp.sum(chosen * local_ids[None, None, :], axis=2)
    return (requests_out, holder_ids * capacity + ranking)


def state_entries(slot_rows, stored_states, group_heads):
    flat_slots = slot_rows.reshape(-1)
    within = jnp.tile(jnp.arange(group_heads, dtype=jnp.int32), flat_slots.shape[0] // group_heads)
    return (flat_slots // stored_states, flat_slots % stored_states * group_heads + within)


def general_body(
    light_query,
    light_key,
    light_value,
    light_gate,
    decay_rate,
    norm_gain,
    state_store,
    state_slot,
    soft_query,
    soft_pair,
    kv_store,
    page_holder,
    page_local,
    prefix_len,
):
    owners = lax.axis_size("pool")
    groups = lax.axis_size("head")
    holders = owners * groups
    requests = prefix_len.shape[0]
    group_heads = decay_rate.shape[0]
    head_width = state_store.shape[-1]
    stored_states = state_store.shape[0]
    stored_pages = kv_store.shape[0]
    key_heads = kv_store.shape[1] // groups
    page_tokens = kv_store.shape[2]
    max_pages = page_local.shape[1]
    suffix = light_query.shape[0] // requests
    state_capacity = max(2, 2 * requests * group_heads // owners)
    page_capacity = max(2, 2 * requests * max_pages // holders)
    state_holders, state_locals = state_entries(state_slot, stored_states, group_heads)
    state_asks, state_picks = plan_lists(state_holders, state_locals, owners, state_capacity)
    page_asks, page_picks = plan_lists(
        page_holder.reshape(-1), page_local.reshape(-1), holders, page_capacity
    )
    state_served = lax.all_to_all(state_asks, "pool", split_axis=0, concat_axis=0, tiled=True)
    page_served = lax.all_to_all(
        page_asks, ("pool", "head"), split_axis=0, concat_axis=0, tiled=True
    )
    flat_states = state_store.reshape(stored_states * group_heads, head_width, head_width)
    outgoing = jnp.take(flat_states, state_served.reshape(-1), axis=0).reshape(
        owners, state_capacity, head_width, head_width
    )
    arrived = lax.all_to_all(outgoing, "pool", split_axis=0, concat_axis=0, tiled=True)
    initial = jnp.take(
        arrived.reshape(owners * state_capacity, head_width, head_width), state_picks, axis=0
    ).reshape(requests, group_heads, head_width, head_width)
    page_rows = kv_store.reshape(stored_pages * groups, key_heads, page_tokens, 2 * head_width)
    target_head = jnp.arange(holders, dtype=jnp.int32) % groups
    wanted = page_served * groups + target_head[:, None]
    outgoing_pages = jnp.take(page_rows, wanted.reshape(-1), axis=0).reshape(
        holders, page_capacity, key_heads, page_tokens, 2 * head_width
    )
    arrived_pages = lax.all_to_all(
        outgoing_pages, ("pool", "head"), split_axis=0, concat_axis=0, tiled=True
    )
    prefix = jnp.take(
        arrived_pages.reshape(holders * page_capacity, key_heads, page_tokens, 2 * head_width),
        page_picks,
        axis=0,
    ).reshape(requests, max_pages, key_heads, page_tokens, 2 * head_width)
    output, updated = lightning(
        light_query.reshape(requests, suffix, group_heads, head_width),
        light_key.reshape(requests, suffix, group_heads, head_width),
        light_value.reshape(requests, suffix, group_heads, head_width),
        decay_rate,
        initial,
    )
    squares = jnp.sum(output * output, axis=(2, 3))
    totals = lax.psum(squares, "head")
    factor = lax.rsqrt(totals / (groups * group_heads * head_width) + 1e-06)
    normed = (
        output.reshape(requests * suffix, group_heads * head_width)
        * factor.reshape(-1, 1)
        * norm_gain
        * jax.nn.sigmoid(light_gate.astype(jnp.float32))
    )
    light_out = normed.astype(jnp.bfloat16)

    def one_request(position):
        first_row = position * suffix
        return attend(
            lax.dynamic_slice_in_dim(soft_query, first_row, suffix, 0),
            lax.dynamic_slice_in_dim(soft_pair, first_row, suffix, 0),
            prefix[position],
            prefix_len[position],
        )

    soft_out = lax.map(one_request, jnp.arange(requests, dtype=jnp.int32)).reshape(
        requests * suffix, group_heads * head_width
    )
    return (light_out, updated, soft_out)


MESH = pl.DeviceIdType.MESH
LANES = 128
CHUNKS = 8
ROW_CAP = 11
STATE_CAP = 4
LOG2E = 1.4426950408889634


def wait_bytes(ref, sem):
    pltpu.make_async_copy(ref, ref, sem).wait()


def make_lists(row_cap, pool, wants, asked, lists, crowd_out):
    i32 = jnp.int32
    lane = lax.broadcasted_iota(i32, (16, LANES), 1)
    row = lax.broadcasted_iota(i32, (16, LANES), 0)
    pages, states = asked[:, 0, :], asked[:, 1, :]
    own_pages = jnp.broadcast_to(wants[0:1, :], (16, LANES))
    own_states = jnp.broadcast_to(wants[1:2, :], (16, LANES))
    page_match = (pages // 128 == pool).astype(i32)
    state_match = (states // 4 == pool).astype(i32)
    own_page_match = (own_pages // 128 == row).astype(i32)
    own_state_match = (own_states // 4 == row).astype(i32)

    def over_lanes(x):
        for shift in (1, 2, 4, 8, 16, 32, 64):
            x = x + pltpu.roll(x, shift, 1)
        return x

    def earlier(x):
        total = x
        for shift in (1, 2, 4, 8, 16, 32, 64):
            total = total + jnp.where(lane >= shift, pltpu.roll(total, shift, 1), 0)
        return total - x

    def picks(match, values, capacity):
        rank = earlier(match)
        found = jnp.zeros((16, LANES), i32)
        for c in range(capacity):
            spot = over_lanes(jnp.where((match == 1) & (rank == c), values, 0))
            found = jnp.where(lane == c, spot, found)
        return found

    def places(match, capacity):
        spot = match * (row * capacity + jnp.minimum(earlier(match), capacity - 1))
        return jnp.broadcast_to(jnp.sum(spot, axis=0, keepdims=True), (1, LANES))

    lists[0:16, :] = picks(page_match, lax.rem(pages, 128), row_cap)
    lists[16:32, :] = picks(state_match, lax.rem(states, 4) * 8 + lax.rem(lane, 8), STATE_CAP)
    lists[32:33, :] = places(own_page_match, row_cap)
    lists[33:34, :] = places(own_state_match, STATE_CAP)
    lists[34:40, :] = jnp.zeros((6, LANES), i32)
    most = jnp.zeros((16, 1), jnp.float32)
    for j in range(16):
        here = (pages // 128 == j).astype(jnp.float32)
        most = jnp.maximum(most, jnp.sum(here, axis=1, keepdims=True))
    crowd_out[...] = jnp.broadcast_to(jnp.max(most, axis=0, keepdims=True), (8, LANES))


def fused_kernel(
    row_cap,
    lengths,
    rates,
    wants,
    q_in,
    k_in,
    v_in,
    gate_in,
    gain_in,
    store_in,
    soft_q,
    pair_in,
    kv_ref,
    light_out,
    state_out,
    soft_out,
    crowd_out,
    a_buf,
    a_cur,
    s_buf,
    r_buf,
    r_cur,
    key_buf,
    val_buf,
    st_send,
    st_recv,
    mix,
    sq_send,
    sq_recv,
    q_cat,
    acc,
    top,
    a_send,
    a_recv,
    b_send,
    b_recv,
    keep_sems,
    st_sems,
    sq_sems,
    asked,
    lists,
    table,
    ask_sems,
    list_sem,
):
    f32, bf16 = jnp.float32, jnp.bfloat16
    tokens = LANES // CHUNKS
    keys = 32 * tokens
    pool, head = lax.axis_index("pool"), lax.axis_index("head")
    px, pz = pool // 4, lax.rem(pool, 4)
    hy, hc = head // 2, lax.rem(head, 2)
    heads_to = [lax.rem(hy + k // 2, 4) * 2 + lax.rem(hc + k % 2, 2) for k in range(1, 8)]
    pools_to = [lax.rem(px + k // 4, 4) * 4 + lax.rem(pz + k % 4, 4) for k in range(1, 16)]

    barrier = pltpu.get_barrier_semaphore()
    for d in heads_to:
        pl.semaphore_signal(barrier, inc=1, device_id={"head": d}, device_id_type=MESH)
    for d in pools_to:
        pl.semaphore_signal(barrier, inc=1, device_id={"pool": d}, device_id_type=MESH)
    pl.semaphore_wait(barrier, 22)

    for d in pools_to:
        pltpu.make_async_remote_copy(
            wants,
            asked.at[pool],
            ask_sems.at[0],
            ask_sems.at[1],
            device_id={"pool": d},
            device_id_type=MESH,
        ).start()
    asked[pool] = wants[...]

    def send_store(t, carry):
        part = pl.ds(pl.multiple_of(t * tokens, tokens), tokens)
        for d in heads_to:
            pltpu.make_async_remote_copy(
                kv_ref.at[:, d, part, :],
                a_buf.at[t, pl.ds(head * 16, 16)],
                a_send.at[t],
                a_recv.at[t],
                device_id={"head": d},
                device_id_type=MESH,
            ).start()
        pltpu.make_async_copy(
            kv_ref.at[:, head, part, :], a_buf.at[t, pl.ds(head * 16, 16)], a_recv.at[t]
        ).start()
        return carry

    lax.fori_loop(0, 2, send_store, 0)

    wait_bytes(asked.at[pl.ds(0, 15)], ask_sems.at[1])
    make_lists(row_cap, pool, wants, asked, lists, crowd_out)
    to_scalars = pltpu.make_async_copy(lists, table, list_sem)
    to_scalars.start()
    to_scalars.wait()

    def pack_state(i, carry):
        for c in range(STATE_CAP):
            st_send[i * STATE_CAP + c] = store_in[table[16 + i, c]].astype(bf16)
        return carry

    lax.fori_loop(0, 16, pack_state, 0)
    mine_st = pl.ds(pool * STATE_CAP, STATE_CAP)
    for d in pools_to:
        pltpu.make_async_remote_copy(
            st_send.at[pl.ds(d * STATE_CAP, STATE_CAP)],
            st_recv.at[mine_st],
            st_sems.at[0],
            st_sems.at[1],
            device_id={"pool": d},
            device_id_type=MESH,
        ).start()
    pltpu.make_async_copy(st_send.at[mine_st], st_recv.at[mine_st], st_sems.at[1]).start()

    lax.fori_loop(2, CHUNKS, send_store, 0)

    temper = LOG2E / math.sqrt(LANES)
    row_i = lax.broadcasted_iota(jnp.int32, (LANES, LANES), 0)
    col_i = lax.broadcasted_iota(jnp.int32, (LANES, LANES), 1)

    def rows_of(r):
        return pl.ds(pl.multiple_of(r * LANES, LANES), LANES)

    def open_softmax(e, carry):
        r, h = e // 8, lax.rem(e, 8)
        q = soft_q[rows_of(r), rows_of(h)]
        q_cat[r, rows_of(h), :] = q
        k = pair_in[rows_of(r), :LANES]
        v = pair_in[rows_of(r), LANES:]
        s = lax.dot_general(q, k, (((1,), (1,)), ((), ())), preferred_element_type=f32) * temper
        s = jnp.where(col_i <= row_i, s, -1e30)
        peak = jnp.max(s, axis=1, keepdims=True)
        p = jnp.exp2(s - peak)
        acc[r, rows_of(h), :LANES] = jnp.dot(p.astype(bf16), v, preferred_element_type=f32)
        acc[r, rows_of(h), LANES:] = p
        top[r, rows_of(h), :] = jnp.broadcast_to(peak, (LANES, LANES))
        return carry

    lax.fori_loop(0, 32, open_softmax, 0)

    lane = lax.broadcasted_iota(jnp.int32, (1, keys), 1)

    def attend_chunk(t):
        wait_bytes(r_buf.at[t, pl.ds(0, 15 * row_cap)], b_recv.at[t])
        wait_bytes(r_buf.at[t, pl.ds(0, row_cap)], keep_sems.at[lax.rem(t, 2)])
        r_cur[...] = r_buf[t]
        spot = (lane // tokens) * LANES + t * tokens + lax.rem(lane, tokens)

        def one_request(r, carry):
            for p in range(32):
                block = r_cur[table[32, r * 32 + p]]
                key_buf[p * tokens : (p + 1) * tokens, :] = block[:, :LANES]
                val_buf[p * tokens : (p + 1) * tokens, :] = block[:, LANES:]
            bias = jnp.where(spot < lengths[r], 0.0, -1e30).astype(f32)

            s = lax.dot_general(
                q_cat[r], key_buf[...], (((1,), (1,)), ((), ())), preferred_element_type=f32
            )
            s = s * temper + bias
            before = top[r]
            peak = jnp.maximum(before, jnp.max(s, axis=1, keepdims=True))
            p = jnp.exp2(s - jnp.concatenate([peak] * (keys // LANES), axis=1))
            shrink = jnp.exp2(before - peak)
            acc[r, :, :LANES] = acc[r, :, :LANES] * shrink + jnp.dot(
                p.astype(bf16), val_buf[...], preferred_element_type=f32
            )
            sums = p[:, :LANES]
            for part in range(1, keys // LANES):
                sums = sums + p[:, part * LANES : (part + 1) * LANES]
            acc[r, :, LANES:] = acc[r, :, LANES:] * shrink + sums
            top[r] = peak
            return carry

        lax.fori_loop(0, 4, one_request, 0)

    def light_request(r):
        spacing = (row_i - col_i).astype(f32)
        steps = lax.broadcasted_iota(jnp.int32, (LANES, 1), 0).astype(f32)

        def one_head(h, total):
            rate = rates[h]
            rows, cols = rows_of(r), rows_of(h)
            q, k, v = q_in[rows, cols], k_in[rows, cols], v_in[rows, cols]
            state = st_recv[table[33, r * 8 + h]]
            weights = jnp.where(spacing >= 0.0, jnp.exp(-rate * jnp.maximum(spacing, 0.0)), 0.0)
            s = lax.dot_general(q, k, (((1,), (1,)), ((), ())), preferred_element_type=f32) * weights
            inside = jnp.dot(s.astype(bf16), v, preferred_element_type=f32)
            carried = jnp.dot(q, state, preferred_element_type=f32) * jnp.exp(-rate * (steps + 1.0))
            out = inside + carried
            mix[rows, cols] = out
            trail = k.astype(f32) * jnp.exp(-rate * (LANES - 1.0 - steps))
            high = trail.astype(bf16)
            low = (trail - high.astype(f32)).astype(bf16)
            across = (((0,), (0,)), ((), ()))
            state_out[r * 8 + h] = (
                state.astype(f32) * jnp.exp(jnp.full((1, 1), -LANES, f32) * rate)
                + lax.dot_general(high, v, across, preferred_element_type=f32)
                + lax.dot_general(low, v, across, preferred_element_type=f32)
            )
            return total + jnp.sum(out * out, axis=1, keepdims=True)

        total = lax.fori_loop(0, 8, one_head, jnp.zeros((LANES, 1), f32))
        sq_send[r] = jnp.broadcast_to(total, (LANES, LANES)).T[:8, :]

    def step(t, carry):
        wait_bytes(a_buf.at[t], a_recv.at[t])
        slot = lax.rem(t, 2)

        @pl.when(t >= 2)
        def _():
            wait_bytes(s_buf.at[slot, pl.ds(0, 15 * row_cap)], b_send.at[slot])

        a_cur[...] = a_buf[t]

        def pack(i, inner):
            for c in range(row_cap):
                s_buf[slot, i * row_cap + c] = a_cur[table[i, c]]
            return inner

        lax.fori_loop(0, 16, pack, 0)
        mine = pl.ds(pool * row_cap, row_cap)
        for d in pools_to:
            pltpu.make_async_remote_copy(
                s_buf.at[slot, pl.ds(d * row_cap, row_cap)],
                r_buf.at[t, mine],
                b_send.at[slot],
                b_recv.at[t],
                device_id={"pool": d},
                device_id_type=MESH,
            ).start()
        pltpu.make_async_copy(s_buf.at[slot, mine], r_buf.at[t, mine], keep_sems.at[slot]).start()

        @pl.when(t == 2)
        def _():
            wait_bytes(st_recv, st_sems.at[1])

        @pl.when((t >= 2) & (t < 6))
        def _():
            light_request(t - 2)

        @pl.when(t == 6)
        def _():
            sq_recv[head] = sq_send[...]
            for d in heads_to:
                pltpu.make_async_remote_copy(
                    sq_send,
                    sq_recv.at[head],
                    sq_sems.at[0],
                    sq_sems.at[1],
                    device_id={"head": d},
                    device_id_type=MESH,
                ).start()

        @pl.when(t >= 1)
        def _():
            attend_chunk(t - 1)

        return carry

    lax.fori_loop(0, CHUNKS, step, 0)
    for slot in range(2):
        wait_bytes(s_buf.at[slot, pl.ds(0, 15 * row_cap)], b_send.at[slot])
    wait_bytes(sq_recv.at[pl.ds(0, 7)], sq_sems.at[1])

    def finish_light(r, carry):
        squares = jnp.sum(sq_recv[:, r, :1, :], axis=0)
        factor = lax.rsqrt(squares / (64.0 * LANES) + 1e-06)
        column = jnp.broadcast_to(factor, (LANES, LANES)).T[:, :1]
        rows = rows_of(r)
        gate = jax.nn.sigmoid(gate_in[rows, :].astype(f32))
        light_out[rows, :] = (mix[rows, :] * column * gain_in[...] * gate).astype(bf16)
        return carry

    lax.fori_loop(0, 4, finish_light, 0)
    attend_chunk(jnp.int32(CHUNKS - 1))

    def finish_soft(e, carry):
        r, h = e // 8, lax.rem(e, 8)
        soft_out[rows_of(r), rows_of(h)] = (
            acc[r, rows_of(h), :LANES] / jnp.sum(acc[r, rows_of(h), LANES:], axis=1, keepdims=True)
        ).astype(bf16)
        return carry

    lax.fori_loop(0, 32, finish_soft, 0)

    def drain(t, carry):
        wait_bytes(a_buf.at[t, pl.ds(0, 112)], a_send.at[t])
        return carry

    lax.fori_loop(0, CHUNKS, drain, 0)
    wait_bytes(st_send.at[pl.ds(0, 15 * STATE_CAP)], st_sems.at[0])
    wait_bytes(sq_recv.at[pl.ds(0, 7)], sq_sems.at[0])
    wait_bytes(asked.at[pl.ds(0, 15)], ask_sems.at[0])


def fused_call(row_cap, lengths, rates, wants, q, k, v, gate, gain, store, soft_q, pair, kv):
    tokens = LANES // CHUNKS
    bf16, f32 = jnp.bfloat16, jnp.float32
    vmem, smem = pl.BlockSpec(memory_space=pltpu.VMEM), pl.BlockSpec(memory_space=pltpu.SMEM)
    dma = pltpu.SemaphoreType.DMA
    return pl.pallas_call(
        functools.partial(fused_kernel, row_cap),
        out_shape=(
            jax.ShapeDtypeStruct((512, 1024), bf16),
            jax.ShapeDtypeStruct((32, LANES, LANES), f32),
            jax.ShapeDtypeStruct((512, 1024), bf16),
            jax.ShapeDtypeStruct((8, LANES), f32),
        ),
        in_specs=[smem, smem] + [vmem] * 9 + [pl.BlockSpec(memory_space=pl.ANY)],
        out_specs=(vmem, vmem, vmem, vmem),
        scratch_shapes=[
            pltpu.VMEM((CHUNKS, 128, tokens, 256), bf16),
            pltpu.VMEM((128, tokens, 256), bf16),
            pltpu.VMEM((2, 16 * row_cap, tokens, 256), bf16),
            pltpu.VMEM((CHUNKS, 16 * row_cap, tokens, 256), bf16),
            pltpu.VMEM((16 * row_cap, tokens, 256), bf16),
            pltpu.VMEM((32 * tokens, LANES), bf16),
            pltpu.VMEM((32 * tokens, LANES), bf16),
            pltpu.VMEM((16 * STATE_CAP, LANES, LANES), bf16),
            pltpu.VMEM((16 * STATE_CAP, LANES, LANES), bf16),
            pltpu.VMEM((512, 1024), f32),
            pltpu.VMEM((4, 8, LANES), f32),
            pltpu.VMEM((8, 4, 8, LANES), f32),
            pltpu.VMEM((4, 1024, LANES), bf16),
            pltpu.VMEM((4, 1024, 2 * LANES), f32),
            pltpu.VMEM((4, 1024, LANES), f32),
            dma((CHUNKS,)),
            dma((CHUNKS,)),
            dma((2,)),
            dma((CHUNKS,)),
            dma((2,)),
            dma((2,)),
            dma((2,)),
            pltpu.VMEM((16, 8, LANES), jnp.int32),
            pltpu.VMEM((40, LANES), jnp.int32),
            pltpu.SMEM((40, LANES), jnp.int32),
            dma((2,)),
            dma,
        ],
        compiler_params=pltpu.CompilerParams(
            collective_id=1, has_side_effects=True, vmem_limit_bytes=60 * 2**20
        ),
        cost_estimate=pl.CostEstimate(flops=10**10, bytes_accessed=3 * 10**7, transcendentals=2 * 10**7),
    )(lengths, rates, wants, q, k, v, gate, gain, store, soft_q, pair, kv)


def wanted(state_slot, page_holder, page_local, prefix_len):
    pages = page_holder[:, :, 0] * 16 + page_local
    active = jnp.arange(32)[None, :] * LANES < prefix_len[:, None]
    own_pages = jnp.where(active, pages, 4095).reshape(1, -1)
    own_states = jnp.pad(state_slot.reshape(1, -1), ((0, 0), (0, 96)), constant_values=255)
    return jnp.concatenate([own_pages, own_states, jnp.zeros((6, LANES), jnp.int32)]).astype(jnp.int32)


def body(
    light_query,
    light_key,
    light_value,
    light_gate,
    decay_rate,
    norm_gain,
    state_store,
    state_slot,
    soft_query,
    soft_pair,
    kv_store,
    page_holder,
    page_local,
    prefix_len,
):
    light, states, soft, crowd = fused_call(
        ROW_CAP,
        prefix_len,
        decay_rate,
        wanted(state_slot, page_holder, page_local, prefix_len),
        light_query,
        light_key,
        light_value,
        light_gate,
        norm_gain.reshape(1, -1),
        state_store.reshape(32, LANES, LANES),
        soft_query,
        soft_pair,
        kv_store,
    )

    def quick():
        return light, states.reshape(4, 8, LANES, LANES), soft

    def general():
        return general_body(
            light_query,
            light_key,
            light_value,
            light_gate,
            decay_rate,
            norm_gain,
            state_store,
            state_slot,
            soft_query,
            soft_pair,
            kv_store,
            page_holder,
            page_local,
            prefix_len,
        )

    return lax.cond(crowd[0, 0] <= ROW_CAP, quick, general)


def solution(mesh):
    return jax.shard_map(
        body,
        mesh=mesh,
        in_specs=(
            P("pool", "head"),
            P("pool", "head"),
            P("pool", "head"),
            P("pool", "head"),
            P("head"),
            P("head"),
            P("pool", "head", None, None),
            P("pool", "head"),
            P("pool", "head"),
            P("pool", "head"),
            P(("pool", "head"), None, None, None),
            P("pool", None, None),
            P("pool", None),
            P("pool"),
        ),
        out_specs=(P("pool", "head"), P("pool", "head", None, None), P("pool", "head")),
        check_vma=False,
    )
```

```python
import functools
import math

import jax
import jax.numpy as jnp
from jax import lax
from jax.experimental import pallas as pl
from jax.experimental.pallas import tpu as pltpu
from jax.sharding import PartitionSpec as P


def lightning(queries, keys_in, values_in, rates_in, initial):
    length = queries.shape[1]
    highest = lax.Precision.HIGHEST
    offsets = jnp.arange(length).astype(jnp.float32)
    spacing = offsets[:, None] - offsets[None, :]
    weights = (
        jnp.exp(-rates_in[:, None, None] * jnp.maximum(spacing, 0.0)[None])
        * (spacing >= 0.0).astype(jnp.float32)[None]
    )
    scores = (
        jnp.einsum("rthd,rshd->rhts", queries, keys_in, preferred_element_type=jnp.float32)
        * weights[None]
    )
    rounded = scores.astype(jnp.bfloat16)
    inside = jnp.einsum("rhts,rshe->rthe", rounded, values_in, preferred_element_type=jnp.float32)
    leading = jnp.exp(-rates_in[None, :] * (offsets[:, None] + 1.0))
    carried = jnp.einsum(
        "rthd,rhde->rthe",
        queries.astype(jnp.float32) * leading[None, :, :, None],
        initial,
        precision=highest,
    )
    trailing = jnp.exp(-rates_in[None, :] * (length - 1.0 - offsets[:, None]))
    updated = jnp.exp(-rates_in * length)[None, :, None, None] * initial + jnp.einsum(
        "rshd,rshe->rhde",
        keys_in.astype(jnp.float32) * trailing[None, :, :, None],
        values_in.astype(jnp.float32),
        precision=highest,
    )
    return (inside + carried, updated)


def attend(query_rows, suffix_kv, prefix_kv, length):
    suffix = query_rows.shape[0]
    key_heads = prefix_kv.shape[1]
    head_width = prefix_kv.shape[-1] // 2
    group_size = query_rows.shape[1] // head_width // key_heads
    grouped = (
        query_rows.reshape(suffix, key_heads, group_size, head_width)
        .transpose(1, 2, 0, 3)
        .reshape(key_heads, group_size * suffix, head_width)
    )
    earlier = prefix_kv.transpose(1, 0, 2, 3).reshape(key_heads, -1, 2 * head_width)
    recent = suffix_kv.reshape(suffix, key_heads, 2 * head_width).transpose(1, 0, 2)
    joined = jnp.concatenate([earlier, recent], axis=1)
    cached_count = earlier.shape[1]
    column = jnp.arange(cached_count + suffix)
    moment = jnp.arange(group_size * suffix) % suffix
    allowed = jnp.where(
        column[None, :] < cached_count,
        column[None, :] < length,
        column[None, :] - cached_count <= moment[:, None],
    )
    temper = 1.0 / math.sqrt(head_width)

    def per_head(operands):
        group_query, group_pair = operands
        scores = (
            jnp.dot(group_query, group_pair[:, :head_width].T, preferred_element_type=jnp.float32)
            * temper
        )
        scores = jnp.where(allowed, scores, -1e30)
        highest = jnp.max(scores, axis=1, keepdims=True)
        lifted = jnp.exp(scores - highest)
        totals = jnp.sum(lifted, axis=1, keepdims=True)
        mixed = jnp.dot(
            lifted.astype(jnp.bfloat16),
            group_pair[:, head_width:],
            preferred_element_type=jnp.float32,
        )
        return mixed / totals

    result = lax.map(per_head, (grouped, joined))
    return (
        result.reshape(key_heads, group_size, suffix, head_width)
        .transpose(2, 0, 1, 3)
        .reshape(suffix, key_heads * group_size * head_width)
        .astype(jnp.bfloat16)
    )


def plan_lists(holder_ids, local_ids, holder_count, capacity):
    matches = (holder_ids[:, None] == jnp.arange(holder_count, dtype=jnp.int32)[None, :]).astype(
        jnp.int32
    )
    before = jnp.cumsum(matches, axis=0) - matches
    ranking = jnp.sum(before * matches, axis=1)
    chosen = matches.T[:, None, :] * (
        ranking[None, None, :] == jnp.arange(capacity, dtype=jnp.int32)[None, :, None]
    ).astype(jnp.int32)
    requests_out = jnp.sum(chosen * local_ids[None, None, :], axis=2)
    return (requests_out, holder_ids * capacity + ranking)


def state_entries(slot_rows, stored_states, group_heads):
    flat_slots = slot_rows.reshape(-1)
    within = jnp.tile(jnp.arange(group_heads, dtype=jnp.int32), flat_slots.shape[0] // group_heads)
    return (flat_slots // stored_states, flat_slots % stored_states * group_heads + within)


def general_body(
    light_query,
    light_key,
    light_value,
    light_gate,
    decay_rate,
    norm_gain,
    state_store,
    state_slot,
    soft_query,
    soft_pair,
    kv_store,
    page_holder,
    page_local,
    prefix_len,
):
    owners = lax.axis_size("pool")
    groups = lax.axis_size("head")
    holders = owners * groups
    requests = prefix_len.shape[0]
    group_heads = decay_rate.shape[0]
    head_width = state_store.shape[-1]
    stored_states = state_store.shape[0]
    stored_pages = kv_store.shape[0]
    key_heads = kv_store.shape[1] // groups
    page_tokens = kv_store.shape[2]
    max_pages = page_local.shape[1]
    suffix = light_query.shape[0] // requests
    state_capacity = max(2, 2 * requests * group_heads // owners)
    page_capacity = max(2, 2 * requests * max_pages // holders)
    state_holders, state_locals = state_entries(state_slot, stored_states, group_heads)
    state_asks, state_picks = plan_lists(state_holders, state_locals, owners, state_capacity)
    page_asks, page_picks = plan_lists(
        page_holder.reshape(-1), page_local.reshape(-1), holders, page_capacity
    )
    state_served = lax.all_to_all(state_asks, "pool", split_axis=0, concat_axis=0, tiled=True)
    page_served = lax.all_to_all(
        page_asks, ("pool", "head"), split_axis=0, concat_axis=0, tiled=True
    )
    flat_states = state_store.reshape(stored_states * group_heads, head_width, head_width)
    outgoing = jnp.take(flat_states, state_served.reshape(-1), axis=0).reshape(
        owners, state_capacity, head_width, head_width
    )
    arrived = lax.all_to_all(outgoing, "pool", split_axis=0, concat_axis=0, tiled=True)
    initial = jnp.take(
        arrived.reshape(owners * state_capacity, head_width, head_width), state_picks, axis=0
    ).reshape(requests, group_heads, head_width, head_width)
    page_rows = kv_store.reshape(stored_pages * groups, key_heads, page_tokens, 2 * head_width)
    target_head = jnp.arange(holders, dtype=jnp.int32) % groups
    wanted = page_served * groups + target_head[:, None]
    outgoing_pages = jnp.take(page_rows, wanted.reshape(-1), axis=0).reshape(
        holders, page_capacity, key_heads, page_tokens, 2 * head_width
    )
    arrived_pages = lax.all_to_all(
        outgoing_pages, ("pool", "head"), split_axis=0, concat_axis=0, tiled=True
    )
    prefix = jnp.take(
        arrived_pages.reshape(holders * page_capacity, key_heads, page_tokens, 2 * head_width),
        page_picks,
        axis=0,
    ).reshape(requests, max_pages, key_heads, page_tokens, 2 * head_width)
    output, updated = lightning(
        light_query.reshape(requests, suffix, group_heads, head_width),
        light_key.reshape(requests, suffix, group_heads, head_width),
        light_value.reshape(requests, suffix, group_heads, head_width),
        decay_rate,
        initial,
    )
    squares = jnp.sum(output * output, axis=(2, 3))
    totals = lax.psum(squares, "head")
    factor = lax.rsqrt(totals / (groups * group_heads * head_width) + 1e-06)
    normed = (
        output.reshape(requests * suffix, group_heads * head_width)
        * factor.reshape(-1, 1)
        * norm_gain
        * jax.nn.sigmoid(light_gate.astype(jnp.float32))
    )
    light_out = normed.astype(jnp.bfloat16)

    def one_request(position):
        first_row = position * suffix
        return attend(
            lax.dynamic_slice_in_dim(soft_query, first_row, suffix, 0),
            lax.dynamic_slice_in_dim(soft_pair, first_row, suffix, 0),
            prefix[position],
            prefix_len[position],
        )

    soft_out = lax.map(one_request, jnp.arange(requests, dtype=jnp.int32)).reshape(
        requests * suffix, group_heads * head_width
    )
    return (light_out, updated, soft_out)


MESH = pl.DeviceIdType.MESH
LANES = 128
CHUNKS = 8
ROW_CAP = 8
EXTRA = 6
STATE_CAP = 4
PIECE = 4
LOG2E = 1.4426950408889634


def wait_bytes(ref, sem):
    pltpu.make_async_copy(ref, ref, sem).wait()


def over_lanes(x):
    for shift in (1, 2, 4, 8, 16, 32, 64):
        x = x + pltpu.roll(x, shift, 1)
    return x


def earlier(x):
    lane = lax.broadcasted_iota(jnp.int32, x.shape, 1)
    total = x
    for shift in (1, 2, 4, 8, 16, 32, 64):
        total = total + jnp.where(lane >= shift, pltpu.roll(total, shift, 1), 0)
    return total - x


def picks(match, rank, values, capacity):
    lane = lax.broadcasted_iota(jnp.int32, match.shape, 1)
    found = jnp.zeros(match.shape, jnp.int32)
    for c in range(capacity):
        spot = over_lanes(jnp.where((match == 1) & (rank == c), values, 0))
        found = jnp.where(lane == c, spot, found)
    return found


def state_lists(pool, wants, asked, lists):
    lane = lax.broadcasted_iota(jnp.int32, (16, LANES), 1)
    row = lax.broadcasted_iota(jnp.int32, (16, LANES), 0)
    states = asked[:, 1, :]
    match = (states // 4 == pool).astype(jnp.int32)
    lists[0:16, :] = picks(match, earlier(match), lax.rem(states, 4) * 8 + lax.rem(lane, 8), STATE_CAP)
    own = (jnp.broadcast_to(wants[1:2, :], (16, LANES)) // 4 == row).astype(jnp.int32)
    spot = own * (row * STATE_CAP + jnp.minimum(earlier(own), STATE_CAP - 1))
    lists[16:24, :] = jnp.broadcast_to(jnp.sum(spot, axis=0, keepdims=True), (8, LANES))


def page_lists(row_cap, pool, wants, asked, lists):
    i32 = jnp.int32
    lane = lax.broadcasted_iota(i32, (16, LANES), 1)
    row = lax.broadcasted_iota(i32, (16, LANES), 0)
    row_x, row_z = row // 4, lax.rem(row, 4)
    pool_z = lax.rem(pool, 4)
    pages = asked[:, 0, :]
    page_rows = pages // 128

    def past(match):
        return jnp.maximum(over_lanes(match) - row_cap, 0)

    def before_z(x):
        return sum(jnp.where(row_z >= k, pltpu.roll(x, k, 0), 0) for k in (1, 2, 3))

    def before_x(x):
        return sum(jnp.where(row_x >= k, pltpu.roll(x, 4 * k, 0), 0) for k in (1, 2, 3))

    match = (page_rows == pool).astype(i32)
    rank = earlier(match)
    slots = lax.rem(pages, 128)
    lists[0:16, :] = picks(match, rank, slots, row_cap)
    spare = jnp.where(rank >= row_cap, before_z(past(match)) + rank - row_cap, -1)
    lists[16:32, :] = picks(match, spare, slots, EXTRA)

    relay = jnp.zeros((16, LANES), i32)
    start = jnp.zeros((16, LANES), i32)
    for x in range(4):
        extra = past((page_rows == x * 4 + pool_z).astype(i32))
        inside = (lane >= start) & (lane < start + extra)
        at = jnp.minimum(before_z(extra) + lane - start, EXTRA - 1)
        relay = jnp.where(inside, x * EXTRA + at, relay)
        start = start + extra
    lists[32:48, :] = relay

    own = (jnp.broadcast_to(wants[0:1, :], (16, LANES)) // 128 == row).astype(i32)
    own_rank = earlier(own)
    beyond = jnp.clip(before_x(past(own)) + own_rank - row_cap, 0, EXTRA - 1)
    spot = own * jnp.where(
        own_rank < row_cap, row * row_cap + own_rank, 16 * row_cap + row_z * EXTRA + beyond
    )

    worst = jnp.zeros((16, LANES), i32)
    for z in range(4):
        along = jnp.zeros((16, LANES), i32)
        for x in range(4):
            extra = past((page_rows == x * 4 + z).astype(i32))
            along = along + extra
            worst = jnp.maximum(worst, before_z(extra) + extra)
        worst = jnp.maximum(worst, along)
    for shift in (1, 2, 4, 8):
        worst = jnp.maximum(worst, pltpu.roll(worst, shift, 0))
    lists[48:49, :] = jnp.broadcast_to(jnp.sum(spot, axis=0, keepdims=True), (1, LANES))
    lists[49:50, :] = worst[0:1, :]
    lists[50:56, :] = jnp.zeros((6, LANES), i32)


def fused_kernel(
    row_cap,
    lengths,
    rates,
    wants,
    gain_in,
    q_hbm,
    k_hbm,
    v_hbm,
    gate_hbm,
    store_hbm,
    soft_q_hbm,
    pair_hbm,
    kv_ref,
    light_hbm,
    state_hbm,
    soft_out,
    crowd_out,
    q_in,
    k_in,
    v_in,
    gate_in,
    pair_in,
    light_out,
    state_out,
    a_buf,
    a_cur,
    s_buf,
    r_buf,
    r_cur,
    key_buf,
    val_buf,
    st_send,
    st_recv,
    mix,
    sq_send,
    sq_recv,
    q_cat,
    acc,
    top,
    a_send,
    a_recv,
    b_send,
    b_recv,
    keep_sems,
    xs_buf,
    xo_buf,
    xo_cur,
    zs_buf,
    x_send,
    x_recv,
    z_send,
    z_recv,
    st_sems,
    sq_sems,
    asked,
    st_lists,
    st_table,
    lists,
    table,
    ask_sems,
    list_sems,
    in_sems,
    out_sems,
):
    f32, bf16 = jnp.float32, jnp.bfloat16
    tokens = LANES // CHUNKS
    keys = 32 * tokens
    pool, head = lax.axis_index("pool"), lax.axis_index("head")
    px, pz = pool // 4, lax.rem(pool, 4)
    hy, hc = head // 2, lax.rem(head, 2)
    heads_to = [lax.rem(hy + k // 2, 4) * 2 + lax.rem(hc + k % 2, 2) for k in range(1, 8)]
    xs_to = [lax.rem(px + k, 4) for k in range(1, 4)]
    zs_to = [lax.rem(pz + k, 4) for k in range(1, 4)]
    pools_to = [lax.rem(px + k // 4, 4) * 4 + lax.rem(pz + k % 4, 4) for k in range(1, 16)]

    def rows_of(r):
        return pl.ds(pl.multiple_of(r * LANES, LANES), LANES)

    load_store = pltpu.make_async_copy(store_hbm, mix, in_sems.at[0])
    load_pair = pltpu.make_async_copy(pair_hbm, pair_in, in_sems.at[1])
    loads = [
        pltpu.make_async_copy(source, target, in_sems.at[2 + n])
        for n, (source, target) in enumerate(
            ((q_hbm, q_in), (k_hbm, k_in), (v_hbm, v_in), (gate_hbm, gate_in))
        )
    ]
    load_store.start()

    def load_query(e, carry):
        r, h = e // 8, lax.rem(e, 8)
        pltpu.make_async_copy(
            soft_q_hbm.at[rows_of(r), rows_of(h)], q_cat.at[r, rows_of(h)], in_sems.at[6]
        ).start()
        return carry

    barrier = pltpu.get_barrier_semaphore()
    for d in heads_to:
        pl.semaphore_signal(barrier, inc=1, device_id={"head": d}, device_id_type=MESH)
    for d in pools_to:
        pl.semaphore_signal(barrier, inc=1, device_id={"pool": d}, device_id_type=MESH)
    pl.semaphore_wait(barrier, 22)

    for d in pools_to:
        pltpu.make_async_remote_copy(
            wants,
            asked.at[pool],
            ask_sems.at[0],
            ask_sems.at[1],
            device_id={"pool": d},
            device_id_type=MESH,
        ).start()
    asked[pool] = wants[...]

    def send_store(t, carry):
        part = pl.ds(pl.multiple_of(t * tokens, tokens), tokens)
        for d in heads_to:
            pltpu.make_async_remote_copy(
                kv_ref.at[:, d, part, :],
                a_buf.at[t, pl.ds(head * 16, 16)],
                a_send.at[t],
                a_recv.at[t],
                device_id={"head": d},
                device_id_type=MESH,
            ).start()
        pltpu.make_async_copy(
            kv_ref.at[:, head, part, :], a_buf.at[t, pl.ds(head * 16, 16)], a_recv.at[t]
        ).start()
        return carry

    lax.fori_loop(0, 2, send_store, 0)

    load_pair.start()
    lax.fori_loop(0, 32, load_query, 0)
    for load in loads:
        load.start()
    wait_bytes(asked.at[pl.ds(0, 15)], ask_sems.at[1])
    state_lists(pool, wants, asked, st_lists)
    to_scalars = pltpu.make_async_copy(st_lists, st_table, list_sems.at[0])
    to_scalars.start()
    to_scalars.wait()

    load_store.wait()

    def pack_state(i, carry):
        for c in range(STATE_CAP):
            st_send[i * STATE_CAP + c] = mix[st_table[i, c]].astype(bf16)
        return carry

    lax.fori_loop(0, 16, pack_state, 0)
    mine_st = pl.ds(pool * STATE_CAP, STATE_CAP)
    for d in pools_to:
        pltpu.make_async_remote_copy(
            st_send.at[pl.ds(d * STATE_CAP, STATE_CAP)],
            st_recv.at[mine_st],
            st_sems.at[0],
            st_sems.at[1],
            device_id={"pool": d},
            device_id_type=MESH,
        ).start()
    pltpu.make_async_copy(st_send.at[mine_st], st_recv.at[mine_st], st_sems.at[1]).start()

    lax.fori_loop(2, CHUNKS, send_store, 0)

    page_lists(row_cap, pool, wants, asked, lists)
    to_table = pltpu.make_async_copy(lists, table, list_sems.at[1])
    to_table.start()
    to_table.wait()
    crowd_out[0, 0] = table[49, 0]

    temper = LOG2E / math.sqrt(LANES)
    row_i = lax.broadcasted_iota(jnp.int32, (LANES, LANES), 0)
    col_i = lax.broadcasted_iota(jnp.int32, (LANES, LANES), 1)

    def open_softmax(e, carry):
        r, h = e // 8, lax.rem(e, 8)
        q = q_cat[r, rows_of(h), :]
        k = pair_in[rows_of(r), :LANES]
        v = pair_in[rows_of(r), LANES:]
        s = lax.dot_general(q, k, (((1,), (1,)), ((), ())), preferred_element_type=f32) * temper
        s = jnp.where(col_i <= row_i, s, -1e30)
        peak = jnp.max(s, axis=1, keepdims=True)
        p = jnp.exp2(s - peak)
        acc[r, rows_of(h), :LANES] = jnp.dot(p.astype(bf16), v, preferred_element_type=f32)
        acc[r, rows_of(h), LANES:] = p
        top[r, rows_of(h), :] = jnp.broadcast_to(peak, (LANES, LANES))
        return carry

    load_pair.wait()
    wait_bytes(q_cat, in_sems.at[6])
    lax.fori_loop(0, 32, open_softmax, 0)

    lane = lax.broadcasted_iota(jnp.int32, (1, keys), 1)

    def attend_chunk(t):
        wait_bytes(r_buf.at[t, pl.ds(0, 15 * row_cap)], b_recv.at[t])
        wait_bytes(r_buf.at[t, pl.ds(0, row_cap)], keep_sems.at[lax.rem(t, 2)])
        wait_bytes(r_buf.at[t, pl.ds(0, 3 * EXTRA)], z_recv.at[t])
        r_cur[...] = r_buf[t]
        spot = (lane // tokens) * LANES + t * tokens + lax.rem(lane, tokens)

        def one_request(r, carry):
            for p in range(32):
                block = r_cur[table[48, r * 32 + p]]
                key_buf[p * tokens : (p + 1) * tokens, :] = block[:, :LANES]
                val_buf[p * tokens : (p + 1) * tokens, :] = block[:, LANES:]
            bias = jnp.where(spot < lengths[r], 0.0, -1e30).astype(f32)

            s = lax.dot_general(
                q_cat[r], key_buf[...], (((1,), (1,)), ((), ())), preferred_element_type=f32
            )
            s = s * temper + bias
            before = top[r]
            peak = jnp.maximum(before, jnp.max(s, axis=1, keepdims=True))
            p = jnp.exp2(s - jnp.concatenate([peak] * (keys // LANES), axis=1))
            shrink = jnp.exp2(before - peak)
            acc[r, :, :LANES] = acc[r, :, :LANES] * shrink + jnp.dot(
                p.astype(bf16), val_buf[...], preferred_element_type=f32
            )
            sums = p[:, :LANES]
            for part in range(1, keys // LANES):
                sums = sums + p[:, part * LANES : (part + 1) * LANES]
            acc[r, :, LANES:] = acc[r, :, LANES:] * shrink + sums
            top[r] = peak
            return carry

        lax.fori_loop(0, 4, one_request, 0)

    def light_request(r):
        spacing = (row_i - col_i).astype(f32)
        steps = lax.broadcasted_iota(jnp.int32, (LANES, 1), 0).astype(f32)

        def one_head(h, total):
            rate = rates[h]
            rows, cols = rows_of(r), rows_of(h)
            q, k, v = q_in[rows, cols], k_in[rows, cols], v_in[rows, cols]
            state = st_recv[st_table[16, r * 8 + h]]
            weights = jnp.where(spacing >= 0.0, jnp.exp(-rate * jnp.maximum(spacing, 0.0)), 0.0)
            s = lax.dot_general(q, k, (((1,), (1,)), ((), ())), preferred_element_type=f32) * weights
            inside = jnp.dot(s.astype(bf16), v, preferred_element_type=f32)
            carried = jnp.dot(q, state, preferred_element_type=f32) * jnp.exp(-rate * (steps + 1.0))
            out = inside + carried
            mix[r * 8 + h] = out
            trail = k.astype(f32) * jnp.exp(-rate * (LANES - 1.0 - steps))
            high = trail.astype(bf16)
            low = (trail - high.astype(f32)).astype(bf16)
            across = (((0,), (0,)), ((), ()))
            state_out[r * 8 + h] = (
                state.astype(f32) * jnp.exp(jnp.full((1, 1), -LANES, f32) * rate)
                + lax.dot_general(high, v, across, preferred_element_type=f32)
                + lax.dot_general(low, v, across, preferred_element_type=f32)
            )
            return total + jnp.sum(out * out, axis=1, keepdims=True)

        total = lax.fori_loop(0, 8, one_head, jnp.zeros((LANES, 1), f32))
        sq_send[r] = jnp.broadcast_to(total, (LANES, LANES)).T[:8, :]

    def step(t, carry):
        wait_bytes(a_buf.at[t], a_recv.at[t])
        slot = lax.rem(t, 2)

        @pl.when(t >= 2)
        def _():
            wait_bytes(s_buf.at[slot, pl.ds(0, 15 * row_cap)], b_send.at[slot])

        a_cur[...] = a_buf[t]

        def along_x(x, e):
            spot = table[16 + 4 * x, e]
            for z in range(1, 4):
                spot = spot + table[16 + 4 * x + z, e]
            return a_cur[spot]

        for e in range(EXTRA):
            for x in range(4):
                xs_buf[t, x * EXTRA + e] = along_x(x, e)
            xo_buf[t, px * EXTRA + e] = along_x(px, e)
        for x in xs_to:
            pltpu.make_async_remote_copy(
                xs_buf.at[t, pl.ds(x * EXTRA, EXTRA)],
                xo_buf.at[t, pl.ds(px * EXTRA, EXTRA)],
                x_send.at[t],
                x_recv.at[t],
                device_id={"pool": x * 4 + pz},
                device_id_type=MESH,
            ).start()

        def pack(i, inner):
            for c in range(row_cap):
                s_buf[slot, i * row_cap + c] = a_cur[table[i, c]]
            return inner

        lax.fori_loop(0, 16, pack, 0)
        mine = pl.ds(pool * row_cap, row_cap)
        for first in range(0, row_cap, PIECE):
            size = min(PIECE, row_cap - first)
            for d in pools_to:
                pltpu.make_async_remote_copy(
                    s_buf.at[slot, pl.ds(d * row_cap + first, size)],
                    r_buf.at[t, pl.ds(pool * row_cap + first, size)],
                    b_send.at[slot],
                    b_recv.at[t],
                    device_id={"pool": d},
                    device_id_type=MESH,
                ).start()
        pltpu.make_async_copy(s_buf.at[slot, mine], r_buf.at[t, mine], keep_sems.at[slot]).start()

        @pl.when(t == 2)
        def _():
            wait_bytes(st_recv, st_sems.at[1])
            for load in loads:
                load.wait()

        @pl.when((t >= 2) & (t < 6))
        def _():
            light_request(t - 2)

        @pl.when(t == 6)
        def _():
            sq_recv[head] = sq_send[...]
            for d in heads_to:
                pltpu.make_async_remote_copy(
                    sq_send,
                    sq_recv.at[head],
                    sq_sems.at[0],
                    sq_sems.at[1],
                    device_id={"head": d},
                    device_id_type=MESH,
                ).start()

        @pl.when(t >= 1)
        def _():
            attend_chunk(t - 1)

        wait_bytes(xo_buf.at[t, pl.ds(0, 3 * EXTRA)], x_recv.at[t])
        xo_cur[...] = xo_buf[t]
        for e in range(EXTRA):
            for z in range(4):
                zs_buf[t, z * EXTRA + e] = xo_cur[table[32 + px * 4 + z, e]]
            r_buf[t, 16 * row_cap + pz * EXTRA + e] = xo_cur[table[32 + pool, e]]
        for z in zs_to:
            pltpu.make_async_remote_copy(
                zs_buf.at[t, pl.ds(z * EXTRA, EXTRA)],
                r_buf.at[t, pl.ds(16 * row_cap + pz * EXTRA, EXTRA)],
                z_send.at[t],
                z_recv.at[t],
                device_id={"pool": px * 4 + z},
                device_id_type=MESH,
            ).start()
        return carry

    lax.fori_loop(0, CHUNKS, step, 0)
    for slot in range(2):
        wait_bytes(s_buf.at[slot, pl.ds(0, 15 * row_cap)], b_send.at[slot])
    wait_bytes(sq_recv.at[pl.ds(0, 7)], sq_sems.at[1])

    def finish_light(r, carry):
        squares = jnp.sum(sq_recv[:, r, :1, :], axis=0)
        factor = lax.rsqrt(squares / (64.0 * LANES) + 1e-06)
        column = jnp.broadcast_to(factor, (LANES, LANES)).T[:, :1]
        rows = rows_of(r)

        def one_head(h, inner):
            cols = rows_of(h)
            gate = jax.nn.sigmoid(gate_in[rows, cols].astype(f32))
            light_out[rows, cols] = (mix[r * 8 + h] * column * gain_in[:, cols] * gate).astype(bf16)
            return inner

        return lax.fori_loop(0, 8, one_head, carry)

    lax.fori_loop(0, 4, finish_light, 0)
    save_light = pltpu.make_async_copy(light_out, light_hbm, out_sems.at[0])
    save_state = pltpu.make_async_copy(state_out, state_hbm, out_sems.at[1])
    save_light.start()
    save_state.start()
    attend_chunk(jnp.int32(CHUNKS - 1))

    def finish_soft(e, carry):
        r, h = e // 8, lax.rem(e, 8)
        soft_out[rows_of(r), rows_of(h)] = (
            acc[r, rows_of(h), :LANES] / jnp.sum(acc[r, rows_of(h), LANES:], axis=1, keepdims=True)
        ).astype(bf16)
        return carry

    lax.fori_loop(0, 32, finish_soft, 0)

    def drain(t, carry):
        wait_bytes(a_buf.at[t, pl.ds(0, 112)], a_send.at[t])
        wait_bytes(xs_buf.at[t, pl.ds(0, 3 * EXTRA)], x_send.at[t])
        wait_bytes(zs_buf.at[t, pl.ds(0, 3 * EXTRA)], z_send.at[t])
        return carry

    lax.fori_loop(0, CHUNKS, drain, 0)
    wait_bytes(st_send.at[pl.ds(0, 15 * STATE_CAP)], st_sems.at[0])
    wait_bytes(sq_recv.at[pl.ds(0, 7)], sq_sems.at[0])
    wait_bytes(asked.at[pl.ds(0, 15)], ask_sems.at[0])
    save_light.wait()
    save_state.wait()


def fused_call(row_cap, lengths, rates, wants, gain, q, k, v, gate, store, soft_q, pair, kv):
    tokens = LANES // CHUNKS
    bf16, f32 = jnp.bfloat16, jnp.float32
    vmem, smem = pl.BlockSpec(memory_space=pltpu.VMEM), pl.BlockSpec(memory_space=pltpu.SMEM)
    hbm = pl.BlockSpec(memory_space=pl.ANY)
    dma = pltpu.SemaphoreType.DMA
    return pl.pallas_call(
        functools.partial(fused_kernel, row_cap),
        out_shape=(
            jax.ShapeDtypeStruct((512, 1024), bf16),
            jax.ShapeDtypeStruct((32, LANES, LANES), f32),
            jax.ShapeDtypeStruct((512, 1024), bf16),
            jax.ShapeDtypeStruct((1, 1), jnp.int32),
        ),
        in_specs=[smem, smem, vmem, vmem] + [hbm] * 8,
        out_specs=(hbm, hbm, vmem, smem),
        scratch_shapes=[
            pltpu.VMEM((512, 1024), bf16),
            pltpu.VMEM((512, 1024), bf16),
            pltpu.VMEM((512, 1024), bf16),
            pltpu.VMEM((512, 1024), bf16),
            pltpu.VMEM((512, 256), bf16),
            pltpu.VMEM((512, 1024), bf16),
            pltpu.VMEM((32, LANES, LANES), f32),
            pltpu.VMEM((CHUNKS, 128, tokens, 256), bf16),
            pltpu.VMEM((128, tokens, 256), bf16),
            pltpu.VMEM((2, 16 * row_cap, tokens, 256), bf16),
            pltpu.VMEM((CHUNKS, 16 * row_cap + 4 * EXTRA, tokens, 256), bf16),
            pltpu.VMEM((16 * row_cap + 4 * EXTRA, tokens, 256), bf16),
            pltpu.VMEM((32 * tokens, LANES), bf16),
            pltpu.VMEM((32 * tokens, LANES), bf16),
            pltpu.VMEM((16 * STATE_CAP, LANES, LANES), bf16),
            pltpu.VMEM((16 * STATE_CAP, LANES, LANES), bf16),
            pltpu.VMEM((32, LANES, LANES), f32),
            pltpu.VMEM((4, 8, LANES), f32),
            pltpu.VMEM((8, 4, 8, LANES), f32),
            pltpu.VMEM((4, 1024, LANES), bf16),
            pltpu.VMEM((4, 1024, 2 * LANES), f32),
            pltpu.VMEM((4, 1024, LANES), f32),
            dma((CHUNKS,)),
            dma((CHUNKS,)),
            dma((2,)),
            dma((CHUNKS,)),
            dma((2,)),
            pltpu.VMEM((CHUNKS, 4 * EXTRA, tokens, 256), bf16),
            pltpu.VMEM((CHUNKS, 4 * EXTRA, tokens, 256), bf16),
            pltpu.VMEM((4 * EXTRA, tokens, 256), bf16),
            pltpu.VMEM((CHUNKS, 4 * EXTRA, tokens, 256), bf16),
            dma((CHUNKS,)),
            dma((CHUNKS,)),
            dma((CHUNKS,)),
            dma((CHUNKS,)),
            dma((2,)),
            dma((2,)),
            pltpu.VMEM((16, 8, LANES), jnp.int32),
            pltpu.VMEM((24, LANES), jnp.int32),
            pltpu.SMEM((24, LANES), jnp.int32),
            pltpu.VMEM((56, LANES), jnp.int32),
            pltpu.SMEM((56, LANES), jnp.int32),
            dma((2,)),
            dma((2,)),
            dma((7,)),
            dma((2,)),
        ],
        compiler_params=pltpu.CompilerParams(
            collective_id=1, has_side_effects=True, vmem_limit_bytes=62 * 2**20
        ),
        cost_estimate=pl.CostEstimate(flops=10**10, bytes_accessed=3 * 10**7, transcendentals=2 * 10**7),
    )(lengths, rates, wants, gain, q, k, v, gate, store, soft_q, pair, kv)


def wanted(state_slot, page_holder, page_local, prefix_len):
    pages = page_holder[:, :, 0] * 16 + page_local
    active = jnp.arange(32)[None, :] * LANES < prefix_len[:, None]
    own_pages = jnp.where(active, pages, 4095).reshape(1, -1)
    own_states = jnp.pad(state_slot.reshape(1, -1), ((0, 0), (0, 96)), constant_values=255)
    return jnp.concatenate([own_pages, own_states, jnp.zeros((6, LANES), jnp.int32)]).astype(jnp.int32)


def body(
    light_query,
    light_key,
    light_value,
    light_gate,
    decay_rate,
    norm_gain,
    state_store,
    state_slot,
    soft_query,
    soft_pair,
    kv_store,
    page_holder,
    page_local,
    prefix_len,
):
    light, states, soft, crowd = fused_call(
        ROW_CAP,
        prefix_len,
        decay_rate,
        wanted(state_slot, page_holder, page_local, prefix_len),
        norm_gain.reshape(1, -1),
        light_query,
        light_key,
        light_value,
        light_gate,
        state_store.reshape(32, LANES, LANES),
        soft_query,
        soft_pair,
        kv_store,
    )

    def quick():
        return light, states.reshape(4, 8, LANES, LANES), soft

    def general():
        return general_body(
            light_query,
            light_key,
            light_value,
            light_gate,
            decay_rate,
            norm_gain,
            state_store,
            state_slot,
            soft_query,
            soft_pair,
            kv_store,
            page_holder,
            page_local,
            prefix_len,
        )

    return lax.cond(crowd[0, 0] <= EXTRA, quick, general)


def solution(mesh):
    return jax.shard_map(
        body,
        mesh=mesh,
        in_specs=(
            P("pool", "head"),
            P("pool", "head"),
            P("pool", "head"),
            P("pool", "head"),
            P("head"),
            P("head"),
            P("pool", "head", None, None),
            P("pool", "head"),
            P("pool", "head"),
            P("pool", "head"),
            P(("pool", "head"), None, None, None),
            P("pool", None, None),
            P("pool", None),
            P("pool"),
        ),
        out_specs=(P("pool", "head"), P("pool", "head", None, None), P("pool", "head")),
        check_vma=False,
    )
```

```python
import functools
import math

import jax
import jax.numpy as jnp
from jax import lax
from jax.experimental import pallas as pl
from jax.experimental.pallas import tpu as pltpu
from jax.sharding import PartitionSpec as P


def lightning(queries, keys_in, values_in, rates_in, initial):
    length = queries.shape[1]
    highest = lax.Precision.HIGHEST
    offsets = jnp.arange(length).astype(jnp.float32)
    spacing = offsets[:, None] - offsets[None, :]
    weights = (
        jnp.exp(-rates_in[:, None, None] * jnp.maximum(spacing, 0.0)[None])
        * (spacing >= 0.0).astype(jnp.float32)[None]
    )
    scores = (
        jnp.einsum("rthd,rshd->rhts", queries, keys_in, preferred_element_type=jnp.float32)
        * weights[None]
    )
    rounded = scores.astype(jnp.bfloat16)
    inside = jnp.einsum("rhts,rshe->rthe", rounded, values_in, preferred_element_type=jnp.float32)
    leading = jnp.exp(-rates_in[None, :] * (offsets[:, None] + 1.0))
    carried = jnp.einsum(
        "rthd,rhde->rthe",
        queries.astype(jnp.float32) * leading[None, :, :, None],
        initial,
        precision=highest,
    )
    trailing = jnp.exp(-rates_in[None, :] * (length - 1.0 - offsets[:, None]))
    updated = jnp.exp(-rates_in * length)[None, :, None, None] * initial + jnp.einsum(
        "rshd,rshe->rhde",
        keys_in.astype(jnp.float32) * trailing[None, :, :, None],
        values_in.astype(jnp.float32),
        precision=highest,
    )
    return (inside + carried, updated)


def attend(query_rows, suffix_kv, prefix_kv, length):
    suffix = query_rows.shape[0]
    key_heads = prefix_kv.shape[1]
    head_width = prefix_kv.shape[-1] // 2
    group_size = query_rows.shape[1] // head_width // key_heads
    grouped = (
        query_rows.reshape(suffix, key_heads, group_size, head_width)
        .transpose(1, 2, 0, 3)
        .reshape(key_heads, group_size * suffix, head_width)
    )
    earlier = prefix_kv.transpose(1, 0, 2, 3).reshape(key_heads, -1, 2 * head_width)
    recent = suffix_kv.reshape(suffix, key_heads, 2 * head_width).transpose(1, 0, 2)
    joined = jnp.concatenate([earlier, recent], axis=1)
    cached_count = earlier.shape[1]
    column = jnp.arange(cached_count + suffix)
    moment = jnp.arange(group_size * suffix) % suffix
    allowed = jnp.where(
        column[None, :] < cached_count,
        column[None, :] < length,
        column[None, :] - cached_count <= moment[:, None],
    )
    temper = 1.0 / math.sqrt(head_width)

    def per_head(operands):
        group_query, group_pair = operands
        scores = (
            jnp.dot(group_query, group_pair[:, :head_width].T, preferred_element_type=jnp.float32)
            * temper
        )
        scores = jnp.where(allowed, scores, -1e30)
        highest = jnp.max(scores, axis=1, keepdims=True)
        lifted = jnp.exp(scores - highest)
        totals = jnp.sum(lifted, axis=1, keepdims=True)
        mixed = jnp.dot(
            lifted.astype(jnp.bfloat16),
            group_pair[:, head_width:],
            preferred_element_type=jnp.float32,
        )
        return mixed / totals

    result = lax.map(per_head, (grouped, joined))
    return (
        result.reshape(key_heads, group_size, suffix, head_width)
        .transpose(2, 0, 1, 3)
        .reshape(suffix, key_heads * group_size * head_width)
        .astype(jnp.bfloat16)
    )


def plan_lists(holder_ids, local_ids, holder_count, capacity):
    matches = (holder_ids[:, None] == jnp.arange(holder_count, dtype=jnp.int32)[None, :]).astype(
        jnp.int32
    )
    before = jnp.cumsum(matches, axis=0) - matches
    ranking = jnp.sum(before * matches, axis=1)
    chosen = matches.T[:, None, :] * (
        ranking[None, None, :] == jnp.arange(capacity, dtype=jnp.int32)[None, :, None]
    ).astype(jnp.int32)
    requests_out = jnp.sum(chosen * local_ids[None, None, :], axis=2)
    return (requests_out, holder_ids * capacity + ranking)


def state_entries(slot_rows, stored_states, group_heads):
    flat_slots = slot_rows.reshape(-1)
    within = jnp.tile(jnp.arange(group_heads, dtype=jnp.int32), flat_slots.shape[0] // group_heads)
    return (flat_slots // stored_states, flat_slots % stored_states * group_heads + within)


def general_body(
    light_query,
    light_key,
    light_value,
    light_gate,
    decay_rate,
    norm_gain,
    state_store,
    state_slot,
    soft_query,
    soft_pair,
    kv_store,
    page_holder,
    page_local,
    prefix_len,
):
    owners = lax.axis_size("pool")
    groups = lax.axis_size("head")
    holders = owners * groups
    requests = prefix_len.shape[0]
    group_heads = decay_rate.shape[0]
    head_width = state_store.shape[-1]
    stored_states = state_store.shape[0]
    stored_pages = kv_store.shape[0]
    key_heads = kv_store.shape[1] // groups
    page_tokens = kv_store.shape[2]
    max_pages = page_local.shape[1]
    suffix = light_query.shape[0] // requests
    state_capacity = max(2, 2 * requests * group_heads // owners)
    page_capacity = max(2, 2 * requests * max_pages // holders)
    state_holders, state_locals = state_entries(state_slot, stored_states, group_heads)
    state_asks, state_picks = plan_lists(state_holders, state_locals, owners, state_capacity)
    page_asks, page_picks = plan_lists(
        page_holder.reshape(-1), page_local.reshape(-1), holders, page_capacity
    )
    state_served = lax.all_to_all(state_asks, "pool", split_axis=0, concat_axis=0, tiled=True)
    page_served = lax.all_to_all(
        page_asks, ("pool", "head"), split_axis=0, concat_axis=0, tiled=True
    )
    flat_states = state_store.reshape(stored_states * group_heads, head_width, head_width)
    outgoing = jnp.take(flat_states, state_served.reshape(-1), axis=0).reshape(
        owners, state_capacity, head_width, head_width
    )
    arrived = lax.all_to_all(outgoing, "pool", split_axis=0, concat_axis=0, tiled=True)
    initial = jnp.take(
        arrived.reshape(owners * state_capacity, head_width, head_width), state_picks, axis=0
    ).reshape(requests, group_heads, head_width, head_width)
    page_rows = kv_store.reshape(stored_pages * groups, key_heads, page_tokens, 2 * head_width)
    target_head = jnp.arange(holders, dtype=jnp.int32) % groups
    wanted = page_served * groups + target_head[:, None]
    outgoing_pages = jnp.take(page_rows, wanted.reshape(-1), axis=0).reshape(
        holders, page_capacity, key_heads, page_tokens, 2 * head_width
    )
    arrived_pages = lax.all_to_all(
        outgoing_pages, ("pool", "head"), split_axis=0, concat_axis=0, tiled=True
    )
    prefix = jnp.take(
        arrived_pages.reshape(holders * page_capacity, key_heads, page_tokens, 2 * head_width),
        page_picks,
        axis=0,
    ).reshape(requests, max_pages, key_heads, page_tokens, 2 * head_width)
    output, updated = lightning(
        light_query.reshape(requests, suffix, group_heads, head_width),
        light_key.reshape(requests, suffix, group_heads, head_width),
        light_value.reshape(requests, suffix, group_heads, head_width),
        decay_rate,
        initial,
    )
    squares = jnp.sum(output * output, axis=(2, 3))
    totals = lax.psum(squares, "head")
    factor = lax.rsqrt(totals / (groups * group_heads * head_width) + 1e-06)
    normed = (
        output.reshape(requests * suffix, group_heads * head_width)
        * factor.reshape(-1, 1)
        * norm_gain
        * jax.nn.sigmoid(light_gate.astype(jnp.float32))
    )
    light_out = normed.astype(jnp.bfloat16)

    def one_request(position):
        first_row = position * suffix
        return attend(
            lax.dynamic_slice_in_dim(soft_query, first_row, suffix, 0),
            lax.dynamic_slice_in_dim(soft_pair, first_row, suffix, 0),
            prefix[position],
            prefix_len[position],
        )

    soft_out = lax.map(one_request, jnp.arange(requests, dtype=jnp.int32)).reshape(
        requests * suffix, group_heads * head_width
    )
    return (light_out, updated, soft_out)


MESH = pl.DeviceIdType.MESH
LANES = 128
CHUNKS = 8
ROW_CAP = 8
EXTRA = 6
STATE_CAP = 4
PIECE = 4
STATE_PIECE = 1
LAG = 2
SLOTS = 2
LOG2E = 1.4426950408889634


def wait_bytes(ref, sem):
    pltpu.make_async_copy(ref, ref, sem).wait()


def over_lanes(x):
    for shift in (1, 2, 4, 8, 16, 32, 64):
        x = x + pltpu.roll(x, shift, 1)
    return x


def earlier(x):
    lane = lax.broadcasted_iota(jnp.int32, x.shape, 1)
    total = x
    for shift in (1, 2, 4, 8, 16, 32, 64):
        total = total + jnp.where(lane >= shift, pltpu.roll(total, shift, 1), 0)
    return total - x


def picks(match, rank, values, capacity):
    lane = lax.broadcasted_iota(jnp.int32, match.shape, 1)
    found = jnp.zeros(match.shape, jnp.int32)
    for c in range(capacity):
        spot = over_lanes(jnp.where((match == 1) & (rank == c), values, 0))
        found = jnp.where(lane == c, spot, found)
    return found


def state_lists(pool, wants, asked, lists):
    lane = lax.broadcasted_iota(jnp.int32, (16, LANES), 1)
    row = lax.broadcasted_iota(jnp.int32, (16, LANES), 0)
    states = asked[:, 1, :]
    match = (states // 4 == pool).astype(jnp.int32)
    lists[0:16, :] = picks(match, earlier(match), lax.rem(states, 4) * 8 + lax.rem(lane, 8), STATE_CAP)
    own = (jnp.broadcast_to(wants[1:2, :], (16, LANES)) // 4 == row).astype(jnp.int32)
    spot = own * (row * STATE_CAP + jnp.minimum(earlier(own), STATE_CAP - 1))
    lists[16:24, :] = jnp.broadcast_to(jnp.sum(spot, axis=0, keepdims=True), (8, LANES))


def page_lists(row_cap, pool, wants, asked, lists):
    i32 = jnp.int32
    lane = lax.broadcasted_iota(i32, (16, LANES), 1)
    row = lax.broadcasted_iota(i32, (16, LANES), 0)
    row_x, row_z = row // 4, lax.rem(row, 4)
    pool_z = lax.rem(pool, 4)
    pages = asked[:, 0, :]
    page_rows = pages // 128

    def past(match):
        return jnp.maximum(over_lanes(match) - row_cap, 0)

    def before_z(x):
        return sum(jnp.where(row_z >= k, pltpu.roll(x, k, 0), 0) for k in (1, 2, 3))

    def before_x(x):
        return sum(jnp.where(row_x >= k, pltpu.roll(x, 4 * k, 0), 0) for k in (1, 2, 3))

    match = (page_rows == pool).astype(i32)
    rank = earlier(match)
    slots = lax.rem(pages, 128)
    lists[0:16, :] = picks(match, rank, slots, row_cap)
    spare = jnp.where(rank >= row_cap, before_z(past(match)) + rank - row_cap, -1)
    lists[16:32, :] = picks(match, spare, slots, EXTRA)

    relay = jnp.zeros((16, LANES), i32)
    start = jnp.zeros((16, LANES), i32)
    for x in range(4):
        extra = past((page_rows == x * 4 + pool_z).astype(i32))
        inside = (lane >= start) & (lane < start + extra)
        at = jnp.minimum(before_z(extra) + lane - start, EXTRA - 1)
        relay = jnp.where(inside, x * EXTRA + at, relay)
        start = start + extra
    lists[32:48, :] = relay

    own = (jnp.broadcast_to(wants[0:1, :], (16, LANES)) // 128 == row).astype(i32)
    own_rank = earlier(own)
    beyond = jnp.clip(before_x(past(own)) + own_rank - row_cap, 0, EXTRA - 1)
    spot = own * jnp.where(
        own_rank < row_cap, row * row_cap + own_rank, 16 * row_cap + row_z * EXTRA + beyond
    )

    worst = jnp.zeros((16, LANES), i32)
    for z in range(4):
        along = jnp.zeros((16, LANES), i32)
        for x in range(4):
            extra = past((page_rows == x * 4 + z).astype(i32))
            along = along + extra
            worst = jnp.maximum(worst, before_z(extra) + extra)
        worst = jnp.maximum(worst, along)
    for shift in (1, 2, 4, 8):
        worst = jnp.maximum(worst, pltpu.roll(worst, shift, 0))
    lists[48:49, :] = jnp.broadcast_to(jnp.sum(spot, axis=0, keepdims=True), (1, LANES))
    lists[49:50, :] = worst[0:1, :]
    lists[50:56, :] = jnp.zeros((6, LANES), i32)


def fused_kernel(
    row_cap,
    lengths,
    rates,
    page_holder,
    page_local,
    state_slot,
    gain_in,
    q_hbm,
    k_hbm,
    v_hbm,
    gate_hbm,
    store_hbm,
    soft_q_hbm,
    pair_hbm,
    kv_ref,
    light_hbm,
    state_hbm,
    soft_out,
    crowd_out,
    q_in,
    k_in,
    v_in,
    gate_in,
    pair_in,
    light_out,
    state_out,
    a_buf,
    a_cur,
    s_buf,
    r_buf,
    r_cur,
    key_buf,
    val_buf,
    st_send,
    st_recv,
    mix,
    sq_send,
    sq_recv,
    q_cat,
    acc,
    top,
    a_send,
    a_recv,
    b_send,
    b_recv,
    xs_buf,
    xo_buf,
    xo_cur,
    zs_buf,
    x_send,
    x_recv,
    z_send,
    z_recv,
    st_sems,
    sq_sems,
    wants,
    asked,
    st_lists,
    st_table,
    lists,
    table,
    ask_sems,
    list_sems,
    in_sems,
    out_sems,
):
    f32, bf16 = jnp.float32, jnp.bfloat16
    tokens = LANES // CHUNKS
    keys = 32 * tokens
    pool, head = lax.axis_index("pool"), lax.axis_index("head")
    px, pz = pool // 4, lax.rem(pool, 4)
    hy, hc = head // 2, lax.rem(head, 2)
    heads_to = [lax.rem(hy + k // 2, 4) * 2 + lax.rem(hc + k % 2, 2) for k in range(1, 8)]
    xs_to = [lax.rem(px + k, 4) for k in range(1, 4)]
    zs_to = [lax.rem(pz + k, 4) for k in range(1, 4)]
    pools_to = [lax.rem(px + k // 4, 4) * 4 + lax.rem(pz + k % 4, 4) for k in range(1, 16)]

    def rows_of(r):
        return pl.ds(pl.multiple_of(r * LANES, LANES), LANES)

    load_store = pltpu.make_async_copy(store_hbm, mix, in_sems.at[0])
    load_pair = pltpu.make_async_copy(pair_hbm, pair_in, in_sems.at[1])
    loads = [
        pltpu.make_async_copy(source, target, in_sems.at[2 + n])
        for n, (source, target) in enumerate(
            ((q_hbm, q_in), (k_hbm, k_in), (v_hbm, v_in), (gate_hbm, gate_in))
        )
    ]
    load_store.start()

    def load_query(e, carry):
        r, h = e // 8, lax.rem(e, 8)
        pltpu.make_async_copy(
            soft_q_hbm.at[rows_of(r), rows_of(h)], q_cat.at[r, rows_of(h)], in_sems.at[6]
        ).start()
        return carry

    page_start = lax.broadcasted_iota(jnp.int32, (1, 32), 1) * LANES
    wants[...] = jnp.full((8, LANES), 4095, jnp.int32)
    for r in range(4):
        ids = page_holder[r : r + 1, :] * 16 + page_local[r : r + 1, :]
        wants[0:1, r * 32 : r * 32 + 32] = jnp.where(page_start < lengths[r], ids, 4095)
        wants[1:2, r * 8 : r * 8 + 8] = state_slot[r : r + 1, :]

    barrier = pltpu.get_barrier_semaphore()
    for d in heads_to:
        pl.semaphore_signal(barrier, inc=1, device_id={"head": d}, device_id_type=MESH)
    for d in pools_to:
        pl.semaphore_signal(barrier, inc=1, device_id={"pool": d}, device_id_type=MESH)
    pl.semaphore_wait(barrier, 22)

    for d in pools_to:
        pltpu.make_async_remote_copy(
            wants,
            asked.at[pool],
            ask_sems.at[0],
            ask_sems.at[1],
            device_id={"pool": d},
            device_id_type=MESH,
        ).start()
    asked[pool] = wants[...]

    def send_store(t, carry):
        part = pl.ds(pl.multiple_of(t * tokens, tokens), tokens)
        for d in heads_to:
            pltpu.make_async_remote_copy(
                kv_ref.at[:, d, part, :],
                a_buf.at[t, pl.ds(head * 16, 16)],
                a_send.at[t],
                a_recv.at[t],
                device_id={"head": d},
                device_id_type=MESH,
            ).start()
        pltpu.make_async_copy(
            kv_ref.at[:, head, part, :], a_buf.at[t, pl.ds(head * 16, 16)], a_recv.at[t]
        ).start()
        return carry

    lax.fori_loop(0, 2, send_store, 0)

    load_pair.start()
    lax.fori_loop(0, 32, load_query, 0)
    for load in loads:
        load.start()
    wait_bytes(asked.at[pl.ds(0, 15)], ask_sems.at[1])
    state_lists(pool, wants, asked, st_lists)
    to_scalars = pltpu.make_async_copy(st_lists, st_table, list_sems.at[0])
    to_scalars.start()
    to_scalars.wait()

    load_store.wait()

    def pack_state(i, carry):
        for c in range(STATE_CAP):
            st_send[i * STATE_CAP + c] = mix[st_table[i, c]].astype(bf16)
        return carry

    lax.fori_loop(0, 16, pack_state, 0)
    mine_st = pl.ds(pool * STATE_CAP, STATE_CAP)
    for first in range(0, STATE_CAP, STATE_PIECE):
        for d in pools_to:
            pltpu.make_async_remote_copy(
                st_send.at[pl.ds(d * STATE_CAP + first, STATE_PIECE)],
                st_recv.at[pl.ds(pool * STATE_CAP + first, STATE_PIECE)],
                st_sems.at[0],
                st_sems.at[1],
                device_id={"pool": d},
                device_id_type=MESH,
            ).start()
    pltpu.make_async_copy(st_send.at[mine_st], st_recv.at[mine_st], st_sems.at[1]).start()

    page_lists(row_cap, pool, wants, asked, lists)
    to_table = pltpu.make_async_copy(lists, table, list_sems.at[1])
    to_table.start()
    lax.fori_loop(2, CHUNKS, send_store, 0)
    to_table.wait()
    crowd_out[0, 0] = table[49, 0]

    temper = LOG2E / math.sqrt(LANES)
    row_i = lax.broadcasted_iota(jnp.int32, (LANES, LANES), 0)
    col_i = lax.broadcasted_iota(jnp.int32, (LANES, LANES), 1)

    def open_softmax(e, carry):
        r, h = e // 8, lax.rem(e, 8)
        q = q_cat[r, rows_of(h), :]
        k = pair_in[rows_of(r), :LANES]
        v = pair_in[rows_of(r), LANES:]
        s = lax.dot_general(q, k, (((1,), (1,)), ((), ())), preferred_element_type=f32) * temper
        s = jnp.where(col_i <= row_i, s, -1e30)
        peak = jnp.max(s, axis=1, keepdims=True)
        p = jnp.exp2(s - peak)
        acc[r, rows_of(h), :LANES] = jnp.dot(p.astype(bf16), v, preferred_element_type=f32)
        acc[r, rows_of(h), LANES:] = p
        top[r, rows_of(h), :] = jnp.broadcast_to(peak, (LANES, LANES))
        return carry


    lane = lax.broadcasted_iota(jnp.int32, (1, keys), 1)

    def attend_chunk(t):
        wait_bytes(r_buf.at[t, pl.ds(0, 15 * row_cap)], b_recv.at[t])
        wait_bytes(r_buf.at[t, pl.ds(0, 3 * EXTRA)], z_recv.at[t])
        r_cur[...] = r_buf[t]
        spot = (lane // tokens) * LANES + t * tokens + lax.rem(lane, tokens)

        def one_request(r, carry):
            for p in range(32):
                block = r_cur[table[48, r * 32 + p]]
                key_buf[p * tokens : (p + 1) * tokens, :] = block[:, :LANES]
                val_buf[p * tokens : (p + 1) * tokens, :] = block[:, LANES:]
            bias = jnp.where(spot < lengths[r], 0.0, -1e30).astype(f32)

            s = lax.dot_general(
                q_cat[r], key_buf[...], (((1,), (1,)), ((), ())), preferred_element_type=f32
            )
            s = s * temper + bias
            before = top[r]
            peak = jnp.maximum(before, jnp.max(s, axis=1, keepdims=True))
            p = jnp.exp2(s - jnp.concatenate([peak] * (keys // LANES), axis=1))
            shrink = jnp.exp2(before - peak)
            acc[r, :, :LANES] = acc[r, :, :LANES] * shrink + jnp.dot(
                p.astype(bf16), val_buf[...], preferred_element_type=f32
            )
            sums = p[:, :LANES]
            for part in range(1, keys // LANES):
                sums = sums + p[:, part * LANES : (part + 1) * LANES]
            acc[r, :, LANES:] = acc[r, :, LANES:] * shrink + sums
            top[r] = peak
            return carry

        lax.fori_loop(0, 4, one_request, 0)

    def light_request(r):
        spacing = (row_i - col_i).astype(f32)
        steps = lax.broadcasted_iota(jnp.int32, (LANES, 1), 0).astype(f32)

        def one_head(h, total):
            rate = rates[h]
            rows, cols = rows_of(r), rows_of(h)
            q, k, v = q_in[rows, cols], k_in[rows, cols], v_in[rows, cols]
            state = st_recv[st_table[16, r * 8 + h]]
            weights = jnp.where(spacing >= 0.0, jnp.exp(-rate * jnp.maximum(spacing, 0.0)), 0.0)
            s = lax.dot_general(q, k, (((1,), (1,)), ((), ())), preferred_element_type=f32) * weights
            inside = jnp.dot(s.astype(bf16), v, preferred_element_type=f32)
            carried = jnp.dot(q, state, preferred_element_type=f32) * jnp.exp(-rate * (steps + 1.0))
            out = inside + carried
            mix[r * 8 + h] = out
            trail = k.astype(f32) * jnp.exp(-rate * (LANES - 1.0 - steps))
            high = trail.astype(bf16)
            low = (trail - high.astype(f32)).astype(bf16)
            across = (((0,), (0,)), ((), ()))
            state_out[r * 8 + h] = (
                state.astype(f32) * jnp.exp(jnp.full((1, 1), -LANES, f32) * rate)
                + lax.dot_general(high, v, across, preferred_element_type=f32)
                + lax.dot_general(low, v, across, preferred_element_type=f32)
            )
            return total + jnp.sum(out * out, axis=1, keepdims=True)

        total = lax.fori_loop(0, 8, one_head, jnp.zeros((LANES, 1), f32))
        sq_send[r] = jnp.broadcast_to(total, (LANES, LANES)).T[:8, :]

    def send_chunk(t):
        wait_bytes(a_buf.at[t], a_recv.at[t])
        slot = lax.rem(t, SLOTS)

        @pl.when(t >= SLOTS)
        def _():
            wait_bytes(s_buf.at[slot, pl.ds(0, 15 * row_cap)], b_send.at[slot])

        a_cur[...] = a_buf[t]

        def along_x(x, e):
            spot = table[16 + 4 * x, e]
            for z in range(1, 4):
                spot = spot + table[16 + 4 * x + z, e]
            return a_cur[spot]

        for e in range(EXTRA):
            for x in range(4):
                xs_buf[t, x * EXTRA + e] = along_x(x, e)
            xo_buf[t, px * EXTRA + e] = along_x(px, e)
        for x in xs_to:
            pltpu.make_async_remote_copy(
                xs_buf.at[t, pl.ds(x * EXTRA, EXTRA)],
                xo_buf.at[t, pl.ds(px * EXTRA, EXTRA)],
                x_send.at[t],
                x_recv.at[t],
                device_id={"pool": x * 4 + pz},
                device_id_type=MESH,
            ).start()

        def pack(i, inner):
            for c in range(row_cap):
                s_buf[slot, i * row_cap + c] = a_cur[table[i, c]]
            return inner

        lax.fori_loop(0, 16, pack, 0)
        for first in range(0, row_cap, PIECE):
            size = min(PIECE, row_cap - first)
            for d in pools_to:
                pltpu.make_async_remote_copy(
                    s_buf.at[slot, pl.ds(d * row_cap + first, size)],
                    r_buf.at[t, pl.ds(pool * row_cap + first, size)],
                    b_send.at[slot],
                    b_recv.at[t],
                    device_id={"pool": d},
                    device_id_type=MESH,
                ).start()
        for c in range(row_cap):
            r_buf[t, pool * row_cap + c] = a_cur[table[pool, c]]

    def relay_chunk(t):
        wait_bytes(xo_buf.at[t, pl.ds(0, 3 * EXTRA)], x_recv.at[t])
        xo_cur[...] = xo_buf[t]
        for e in range(EXTRA):
            for z in range(4):
                zs_buf[t, z * EXTRA + e] = xo_cur[table[32 + px * 4 + z, e]]
            r_buf[t, 16 * row_cap + pz * EXTRA + e] = xo_cur[table[32 + pool, e]]
        for z in zs_to:
            pltpu.make_async_remote_copy(
                zs_buf.at[t, pl.ds(z * EXTRA, EXTRA)],
                r_buf.at[t, pl.ds(16 * row_cap + pz * EXTRA, EXTRA)],
                z_send.at[t],
                z_recv.at[t],
                device_id={"pool": px * 4 + z},
                device_id_type=MESH,
            ).start()


    def finish_light(r, carry):
        squares = jnp.sum(sq_recv[:, r, :1, :], axis=0)
        factor = lax.rsqrt(squares / (64.0 * LANES) + 1e-06)
        column = jnp.broadcast_to(factor, (LANES, LANES)).T[:, :1]
        rows = rows_of(r)

        def one_head(h, inner):
            cols = rows_of(h)
            gate = jax.nn.sigmoid(gate_in[rows, cols].astype(f32))
            light_out[rows, cols] = (mix[r * 8 + h] * column * gain_in[:, cols] * gate).astype(bf16)
            return inner

        return lax.fori_loop(0, 8, one_head, carry)

    save_light = pltpu.make_async_copy(light_out, light_hbm, out_sems.at[0])
    save_state = pltpu.make_async_copy(state_out, state_hbm, out_sems.at[1])

    def step(t, carry):
        @pl.when(t < CHUNKS)
        def _():
            send_chunk(t)

        @pl.when(t == 0)
        def _():
            load_pair.wait()
            wait_bytes(q_cat, in_sems.at[6])
            lax.fori_loop(0, 32, open_softmax, 0)

        @pl.when((t >= 1) & (t <= CHUNKS))
        def _():
            relay_chunk(t - 1)

        @pl.when(t == 2)
        def _():
            wait_bytes(st_recv, st_sems.at[1])
            for load in loads:
                load.wait()

        @pl.when((t >= 2) & (t < 6))
        def _():
            light_request(t - 2)

        @pl.when(t == 6)
        def _():
            sq_recv[head] = sq_send[...]
            for d in heads_to:
                pltpu.make_async_remote_copy(
                    sq_send,
                    sq_recv.at[head],
                    sq_sems.at[0],
                    sq_sems.at[1],
                    device_id={"head": d},
                    device_id_type=MESH,
                ).start()

        @pl.when(t == CHUNKS)
        def _():
            wait_bytes(sq_recv.at[pl.ds(0, 7)], sq_sems.at[1])
            lax.fori_loop(0, 4, finish_light, 0)
            save_light.start()
            save_state.start()

        @pl.when(t >= LAG)
        def _():
            attend_chunk(t - LAG)

        return carry


    lax.fori_loop(0, CHUNKS + LAG, step, 0)

    def finish_soft(e, carry):
        r, h = e // 8, lax.rem(e, 8)
        soft_out[rows_of(r), rows_of(h)] = (
            acc[r, rows_of(h), :LANES] / jnp.sum(acc[r, rows_of(h), LANES:], axis=1, keepdims=True)
        ).astype(bf16)
        return carry

    lax.fori_loop(0, 32, finish_soft, 0)

    def drain(t, carry):
        wait_bytes(a_buf.at[t, pl.ds(0, 112)], a_send.at[t])
        wait_bytes(xs_buf.at[t, pl.ds(0, 3 * EXTRA)], x_send.at[t])
        wait_bytes(zs_buf.at[t, pl.ds(0, 3 * EXTRA)], z_send.at[t])
        return carry

    lax.fori_loop(0, CHUNKS, drain, 0)
    for slot in range(SLOTS):
        wait_bytes(s_buf.at[slot, pl.ds(0, 15 * row_cap)], b_send.at[slot])
    wait_bytes(st_send.at[pl.ds(0, 15 * STATE_CAP)], st_sems.at[0])
    wait_bytes(sq_recv.at[pl.ds(0, 7)], sq_sems.at[0])
    wait_bytes(asked.at[pl.ds(0, 15)], ask_sems.at[0])
    save_light.wait()
    save_state.wait()


def fused_call(row_cap, lengths, rates, page_holder, page_local, state_slot, gain, q, k, v, gate, store, soft_q, pair, kv):
    tokens = LANES // CHUNKS
    bf16, f32 = jnp.bfloat16, jnp.float32
    vmem, smem = pl.BlockSpec(memory_space=pltpu.VMEM), pl.BlockSpec(memory_space=pltpu.SMEM)
    hbm = pl.BlockSpec(memory_space=pl.ANY)
    dma = pltpu.SemaphoreType.DMA
    return pl.pallas_call(
        functools.partial(fused_kernel, row_cap),
        out_shape=(
            jax.ShapeDtypeStruct((512, 1024), bf16),
            jax.ShapeDtypeStruct((32, LANES, LANES), f32),
            jax.ShapeDtypeStruct((512, 1024), bf16),
            jax.ShapeDtypeStruct((1, 1), jnp.int32),
        ),
        in_specs=[smem, smem, vmem, vmem, vmem, vmem] + [hbm] * 8,
        out_specs=(hbm, hbm, vmem, smem),
        scratch_shapes=[
            pltpu.VMEM((512, 1024), bf16),
            pltpu.VMEM((512, 1024), bf16),
            pltpu.VMEM((512, 1024), bf16),
            pltpu.VMEM((512, 1024), bf16),
            pltpu.VMEM((512, 256), bf16),
            pltpu.VMEM((512, 1024), bf16),
            pltpu.VMEM((32, LANES, LANES), f32),
            pltpu.VMEM((CHUNKS, 128, tokens, 256), bf16),
            pltpu.VMEM((128, tokens, 256), bf16),
            pltpu.VMEM((SLOTS, 16 * row_cap, tokens, 256), bf16),
            pltpu.VMEM((CHUNKS, 16 * row_cap + 4 * EXTRA, tokens, 256), bf16),
            pltpu.VMEM((16 * row_cap + 4 * EXTRA, tokens, 256), bf16),
            pltpu.VMEM((32 * tokens, LANES), bf16),
            pltpu.VMEM((32 * tokens, LANES), bf16),
            pltpu.VMEM((16 * STATE_CAP, LANES, LANES), bf16),
            pltpu.VMEM((16 * STATE_CAP, LANES, LANES), bf16),
            pltpu.VMEM((32, LANES, LANES), f32),
            pltpu.VMEM((4, 8, LANES), f32),
            pltpu.VMEM((8, 4, 8, LANES), f32),
            pltpu.VMEM((4, 1024, LANES), bf16),
            pltpu.VMEM((4, 1024, 2 * LANES), f32),
            pltpu.VMEM((4, 1024, LANES), f32),
            dma((CHUNKS,)),
            dma((CHUNKS,)),
            dma((SLOTS,)),
            dma((CHUNKS,)),
            pltpu.VMEM((CHUNKS, 4 * EXTRA, tokens, 256), bf16),
            pltpu.VMEM((CHUNKS, 4 * EXTRA, tokens, 256), bf16),
            pltpu.VMEM((4 * EXTRA, tokens, 256), bf16),
            pltpu.VMEM((CHUNKS, 4 * EXTRA, tokens, 256), bf16),
            dma((CHUNKS,)),
            dma((CHUNKS,)),
            dma((CHUNKS,)),
            dma((CHUNKS,)),
            dma((2,)),
            dma((2,)),
            pltpu.VMEM((8, LANES), jnp.int32),
            pltpu.VMEM((16, 8, LANES), jnp.int32),
            pltpu.VMEM((24, LANES), jnp.int32),
            pltpu.SMEM((24, LANES), jnp.int32),
            pltpu.VMEM((56, LANES), jnp.int32),
            pltpu.SMEM((56, LANES), jnp.int32),
            dma((2,)),
            dma((2,)),
            dma((7,)),
            dma((2,)),
        ],
        compiler_params=pltpu.CompilerParams(
            collective_id=1, has_side_effects=True, vmem_limit_bytes=63 * 2**20
        ),
        cost_estimate=pl.CostEstimate(flops=10**10, bytes_accessed=3 * 10**7, transcendentals=2 * 10**7),
    )(lengths, rates, page_holder, page_local, state_slot, gain, q, k, v, gate, store, soft_q, pair, kv)


def keep_kernel(*refs):
    half = len(refs) // 2
    for n in range(half):
        refs[half + n][...] = refs[n][...]


def keep_results(*arrays):
    steps = 4
    specs = [
        pl.BlockSpec(
            (x.shape[0] // steps,) + x.shape[1:], lambda i, rank=x.ndim: (i,) + (0,) * (rank - 1)
        )
        for x in arrays
    ]
    return pl.pallas_call(
        keep_kernel,
        grid=(steps,),
        out_shape=tuple(jax.ShapeDtypeStruct(x.shape, x.dtype) for x in arrays),
        in_specs=specs,
        out_specs=tuple(specs),
        compiler_params=pltpu.CompilerParams(vmem_limit_bytes=16 * 2**20),
    )(*arrays)


def body(
    light_query,
    light_key,
    light_value,
    light_gate,
    decay_rate,
    norm_gain,
    state_store,
    state_slot,
    soft_query,
    soft_pair,
    kv_store,
    page_holder,
    page_local,
    prefix_len,
):
    light, states, soft, crowd = fused_call(
        ROW_CAP,
        prefix_len,
        decay_rate,
        page_holder.reshape(4, 32),
        page_local,
        state_slot,
        norm_gain.reshape(1, -1),
        light_query,
        light_key,
        light_value,
        light_gate,
        state_store.reshape(32, LANES, LANES),
        soft_query,
        soft_pair,
        kv_store,
    )

    def quick():
        kept = keep_results(light, states, soft)
        return kept[0], kept[1].reshape(4, 8, LANES, LANES), kept[2]

    def general():
        return general_body(
            light_query,
            light_key,
            light_value,
            light_gate,
            decay_rate,
            norm_gain,
            state_store,
            state_slot,
            soft_query,
            soft_pair,
            kv_store,
            page_holder,
            page_local,
            prefix_len,
        )

    return lax.cond(crowd[0, 0] <= EXTRA, quick, general)


def solution(mesh):
    return jax.shard_map(
        body,
        mesh=mesh,
        in_specs=(
            P("pool", "head"),
            P("pool", "head"),
            P("pool", "head"),
            P("pool", "head"),
            P("head"),
            P("head"),
            P("pool", "head", None, None),
            P("pool", "head"),
            P("pool", "head"),
            P("pool", "head"),
            P(("pool", "head"), None, None, None),
            P("pool", None, None),
            P("pool", None),
            P("pool"),
        ),
        out_specs=(P("pool", "head"), P("pool", "head", None, None), P("pool", "head")),
        check_vma=False,
    )
```

```python
import functools
import math

import jax
import jax.numpy as jnp
from jax import lax
from jax.experimental import pallas as pl
from jax.experimental.pallas import tpu as pltpu
from jax.sharding import PartitionSpec as P


def lightning(queries, keys_in, values_in, rates_in, initial):
    length = queries.shape[1]
    highest = lax.Precision.HIGHEST
    offsets = jnp.arange(length).astype(jnp.float32)
    spacing = offsets[:, None] - offsets[None, :]
    weights = (
        jnp.exp(-rates_in[:, None, None] * jnp.maximum(spacing, 0.0)[None])
        * (spacing >= 0.0).astype(jnp.float32)[None]
    )
    scores = (
        jnp.einsum("rthd,rshd->rhts", queries, keys_in, preferred_element_type=jnp.float32)
        * weights[None]
    )
    rounded = scores.astype(jnp.bfloat16)
    inside = jnp.einsum("rhts,rshe->rthe", rounded, values_in, preferred_element_type=jnp.float32)
    leading = jnp.exp(-rates_in[None, :] * (offsets[:, None] + 1.0))
    carried = jnp.einsum(
        "rthd,rhde->rthe",
        queries.astype(jnp.float32) * leading[None, :, :, None],
        initial,
        precision=highest,
    )
    trailing = jnp.exp(-rates_in[None, :] * (length - 1.0 - offsets[:, None]))
    updated = jnp.exp(-rates_in * length)[None, :, None, None] * initial + jnp.einsum(
        "rshd,rshe->rhde",
        keys_in.astype(jnp.float32) * trailing[None, :, :, None],
        values_in.astype(jnp.float32),
        precision=highest,
    )
    return (inside + carried, updated)


def attend(query_rows, suffix_kv, prefix_kv, length):
    suffix = query_rows.shape[0]
    key_heads = prefix_kv.shape[1]
    head_width = prefix_kv.shape[-1] // 2
    group_size = query_rows.shape[1] // head_width // key_heads
    grouped = (
        query_rows.reshape(suffix, key_heads, group_size, head_width)
        .transpose(1, 2, 0, 3)
        .reshape(key_heads, group_size * suffix, head_width)
    )
    earlier = prefix_kv.transpose(1, 0, 2, 3).reshape(key_heads, -1, 2 * head_width)
    recent = suffix_kv.reshape(suffix, key_heads, 2 * head_width).transpose(1, 0, 2)
    joined = jnp.concatenate([earlier, recent], axis=1)
    cached_count = earlier.shape[1]
    column = jnp.arange(cached_count + suffix)
    moment = jnp.arange(group_size * suffix) % suffix
    allowed = jnp.where(
        column[None, :] < cached_count,
        column[None, :] < length,
        column[None, :] - cached_count <= moment[:, None],
    )
    temper = 1.0 / math.sqrt(head_width)

    def per_head(operands):
        group_query, group_pair = operands
        scores = (
            jnp.dot(group_query, group_pair[:, :head_width].T, preferred_element_type=jnp.float32)
            * temper
        )
        scores = jnp.where(allowed, scores, -1e30)
        highest = jnp.max(scores, axis=1, keepdims=True)
        lifted = jnp.exp(scores - highest)
        totals = jnp.sum(lifted, axis=1, keepdims=True)
        mixed = jnp.dot(
            lifted.astype(jnp.bfloat16),
            group_pair[:, head_width:],
            preferred_element_type=jnp.float32,
        )
        return mixed / totals

    result = lax.map(per_head, (grouped, joined))
    return (
        result.reshape(key_heads, group_size, suffix, head_width)
        .transpose(2, 0, 1, 3)
        .reshape(suffix, key_heads * group_size * head_width)
        .astype(jnp.bfloat16)
    )


def plan_lists(holder_ids, local_ids, holder_count, capacity):
    matches = (holder_ids[:, None] == jnp.arange(holder_count, dtype=jnp.int32)[None, :]).astype(
        jnp.int32
    )
    before = jnp.cumsum(matches, axis=0) - matches
    ranking = jnp.sum(before * matches, axis=1)
    chosen = matches.T[:, None, :] * (
        ranking[None, None, :] == jnp.arange(capacity, dtype=jnp.int32)[None, :, None]
    ).astype(jnp.int32)
    requests_out = jnp.sum(chosen * local_ids[None, None, :], axis=2)
    return (requests_out, holder_ids * capacity + ranking)


def state_entries(slot_rows, stored_states, group_heads):
    flat_slots = slot_rows.reshape(-1)
    within = jnp.tile(jnp.arange(group_heads, dtype=jnp.int32), flat_slots.shape[0] // group_heads)
    return (flat_slots // stored_states, flat_slots % stored_states * group_heads + within)


def general_body(
    light_query,
    light_key,
    light_value,
    light_gate,
    decay_rate,
    norm_gain,
    state_store,
    state_slot,
    soft_query,
    soft_pair,
    kv_store,
    page_holder,
    page_local,
    prefix_len,
):
    owners = lax.axis_size("pool")
    groups = lax.axis_size("head")
    holders = owners * groups
    requests = prefix_len.shape[0]
    group_heads = decay_rate.shape[0]
    head_width = state_store.shape[-1]
    stored_states = state_store.shape[0]
    stored_pages = kv_store.shape[0]
    key_heads = kv_store.shape[1] // groups
    page_tokens = kv_store.shape[2]
    max_pages = page_local.shape[1]
    suffix = light_query.shape[0] // requests
    state_capacity = max(2, 2 * requests * group_heads // owners)
    page_capacity = max(2, 2 * requests * max_pages // holders)
    state_holders, state_locals = state_entries(state_slot, stored_states, group_heads)
    state_asks, state_picks = plan_lists(state_holders, state_locals, owners, state_capacity)
    page_asks, page_picks = plan_lists(
        page_holder.reshape(-1), page_local.reshape(-1), holders, page_capacity
    )
    state_served = lax.all_to_all(state_asks, "pool", split_axis=0, concat_axis=0, tiled=True)
    page_served = lax.all_to_all(
        page_asks, ("pool", "head"), split_axis=0, concat_axis=0, tiled=True
    )
    flat_states = state_store.reshape(stored_states * group_heads, head_width, head_width)
    outgoing = jnp.take(flat_states, state_served.reshape(-1), axis=0).reshape(
        owners, state_capacity, head_width, head_width
    )
    arrived = lax.all_to_all(outgoing, "pool", split_axis=0, concat_axis=0, tiled=True)
    initial = jnp.take(
        arrived.reshape(owners * state_capacity, head_width, head_width), state_picks, axis=0
    ).reshape(requests, group_heads, head_width, head_width)
    page_rows = kv_store.reshape(stored_pages * groups, key_heads, page_tokens, 2 * head_width)
    target_head = jnp.arange(holders, dtype=jnp.int32) % groups
    wanted = page_served * groups + target_head[:, None]
    outgoing_pages = jnp.take(page_rows, wanted.reshape(-1), axis=0).reshape(
        holders, page_capacity, key_heads, page_tokens, 2 * head_width
    )
    arrived_pages = lax.all_to_all(
        outgoing_pages, ("pool", "head"), split_axis=0, concat_axis=0, tiled=True
    )
    prefix = jnp.take(
        arrived_pages.reshape(holders * page_capacity, key_heads, page_tokens, 2 * head_width),
        page_picks,
        axis=0,
    ).reshape(requests, max_pages, key_heads, page_tokens, 2 * head_width)
    output, updated = lightning(
        light_query.reshape(requests, suffix, group_heads, head_width),
        light_key.reshape(requests, suffix, group_heads, head_width),
        light_value.reshape(requests, suffix, group_heads, head_width),
        decay_rate,
        initial,
    )
    squares = jnp.sum(output * output, axis=(2, 3))
    totals = lax.psum(squares, "head")
    factor = lax.rsqrt(totals / (groups * group_heads * head_width) + 1e-06)
    normed = (
        output.reshape(requests * suffix, group_heads * head_width)
        * factor.reshape(-1, 1)
        * norm_gain
        * jax.nn.sigmoid(light_gate.astype(jnp.float32))
    )
    light_out = normed.astype(jnp.bfloat16)

    def one_request(position):
        first_row = position * suffix
        return attend(
            lax.dynamic_slice_in_dim(soft_query, first_row, suffix, 0),
            lax.dynamic_slice_in_dim(soft_pair, first_row, suffix, 0),
            prefix[position],
            prefix_len[position],
        )

    soft_out = lax.map(one_request, jnp.arange(requests, dtype=jnp.int32)).reshape(
        requests * suffix, group_heads * head_width
    )
    return (light_out, updated, soft_out)


MESH = pl.DeviceIdType.MESH
LANES = 128
CHUNKS = 8
ROW_CAP = 8
EXTRA = 6
STATE_CAP = 4
PIECE = 4
STATE_PIECE = 1
LAG = 2
SLOTS = 2
LOG2E = 1.4426950408889634


def wait_bytes(ref, sem):
    pltpu.make_async_copy(ref, ref, sem).wait()


def over_lanes(x):
    for shift in (1, 2, 4, 8, 16, 32, 64):
        x = x + pltpu.roll(x, shift, 1)
    return x


def earlier(x):
    lane = lax.broadcasted_iota(jnp.int32, x.shape, 1)
    total = x
    for shift in (1, 2, 4, 8, 16, 32, 64):
        total = total + jnp.where(lane >= shift, pltpu.roll(total, shift, 1), 0)
    return total - x


def picks(match, rank, values, capacity):
    lane = lax.broadcasted_iota(jnp.int32, match.shape, 1)
    found = jnp.zeros(match.shape, jnp.int32)
    for c in range(capacity):
        spot = over_lanes(jnp.where((match == 1) & (rank == c), values, 0))
        found = jnp.where(lane == c, spot, found)
    return found


def state_lists(pool, wants, asked, lists):
    lane = lax.broadcasted_iota(jnp.int32, (16, LANES), 1)
    row = lax.broadcasted_iota(jnp.int32, (16, LANES), 0)
    states = asked[:, 1, :]
    match = (states // 4 == pool).astype(jnp.int32)
    lists[0:16, :] = picks(match, earlier(match), lax.rem(states, 4) * 8 + lax.rem(lane, 8), STATE_CAP)
    own = (jnp.broadcast_to(wants[1:2, :], (16, LANES)) // 4 == row).astype(jnp.int32)
    spot = own * (row * STATE_CAP + jnp.minimum(earlier(own), STATE_CAP - 1))
    lists[16:24, :] = jnp.broadcast_to(jnp.sum(spot, axis=0, keepdims=True), (8, LANES))


def page_lists(row_cap, pool, wants, asked, lists):
    i32 = jnp.int32
    lane = lax.broadcasted_iota(i32, (16, LANES), 1)
    row = lax.broadcasted_iota(i32, (16, LANES), 0)
    row_x, row_z = row // 4, lax.rem(row, 4)
    pool_z = lax.rem(pool, 4)
    pages = asked[:, 0, :]
    page_rows = pages // 128

    def past(match):
        return jnp.maximum(over_lanes(match) - row_cap, 0)

    def before_z(x):
        return sum(jnp.where(row_z >= k, pltpu.roll(x, k, 0), 0) for k in (1, 2, 3))

    def before_x(x):
        return sum(jnp.where(row_x >= k, pltpu.roll(x, 4 * k, 0), 0) for k in (1, 2, 3))

    match = (page_rows == pool).astype(i32)
    rank = earlier(match)
    slots = lax.rem(pages, 128)
    lists[0:16, :] = picks(match, rank, slots, row_cap)
    spare = jnp.where(rank >= row_cap, before_z(past(match)) + rank - row_cap, -1)
    lists[16:32, :] = picks(match, spare, slots, EXTRA)

    relay = jnp.zeros((16, LANES), i32)
    start = jnp.zeros((16, LANES), i32)
    for x in range(4):
        extra = past((page_rows == x * 4 + pool_z).astype(i32))
        inside = (lane >= start) & (lane < start + extra)
        at = jnp.minimum(before_z(extra) + lane - start, EXTRA - 1)
        relay = jnp.where(inside, x * EXTRA + at, relay)
        start = start + extra
    lists[32:48, :] = relay

    own = (jnp.broadcast_to(wants[0:1, :], (16, LANES)) // 128 == row).astype(i32)
    own_rank = earlier(own)
    beyond = jnp.clip(before_x(past(own)) + own_rank - row_cap, 0, EXTRA - 1)
    spot = own * jnp.where(
        own_rank < row_cap, row * row_cap + own_rank, 16 * row_cap + row_z * EXTRA + beyond
    )

    worst = jnp.zeros((16, LANES), i32)
    for z in range(4):
        along = jnp.zeros((16, LANES), i32)
        for x in range(4):
            extra = past((page_rows == x * 4 + z).astype(i32))
            along = along + extra
            worst = jnp.maximum(worst, before_z(extra) + extra)
        worst = jnp.maximum(worst, along)
    for shift in (1, 2, 4, 8):
        worst = jnp.maximum(worst, pltpu.roll(worst, shift, 0))
    lists[48:49, :] = jnp.broadcast_to(jnp.sum(spot, axis=0, keepdims=True), (1, LANES))
    lists[49:50, :] = worst[0:1, :]
    lists[50:56, :] = jnp.zeros((6, LANES), i32)


def fused_kernel(
    row_cap,
    lengths,
    rates,
    page_holder,
    page_local,
    state_slot,
    gain_in,
    q_hbm,
    k_hbm,
    v_hbm,
    gate_hbm,
    store_hbm,
    soft_q_hbm,
    pair_hbm,
    kv_ref,
    light_hbm,
    state_hbm,
    soft_out,
    crowd_out,
    q_in,
    k_in,
    v_in,
    gate_in,
    pair_in,
    light_out,
    state_out,
    a_buf,
    a_cur,
    s_buf,
    r_buf,
    r_cur,
    key_buf,
    val_buf,
    st_send,
    st_recv,
    mix,
    sq_send,
    sq_recv,
    q_cat,
    acc,
    top,
    a_send,
    a_recv,
    b_send,
    b_recv,
    xs_buf,
    xo_buf,
    xo_cur,
    zs_buf,
    x_send,
    x_recv,
    z_send,
    z_recv,
    st_sems,
    sq_sems,
    wants,
    asked,
    st_lists,
    st_table,
    lists,
    table,
    ask_sems,
    list_sems,
    in_sems,
    out_sems,
):
    f32, bf16 = jnp.float32, jnp.bfloat16
    tokens = LANES // CHUNKS
    keys = 32 * tokens
    pool, head = lax.axis_index("pool"), lax.axis_index("head")
    px, pz = pool // 4, lax.rem(pool, 4)
    hy, hc = head // 2, lax.rem(head, 2)
    heads_to = [lax.rem(hy + k // 2, 4) * 2 + lax.rem(hc + k % 2, 2) for k in range(1, 8)]
    xs_to = [lax.rem(px + k, 4) for k in range(1, 4)]
    zs_to = [lax.rem(pz + k, 4) for k in range(1, 4)]
    turn = (1 + 2 * hc)
    pools_to = [
        lax.rem(px + dx * turn, 4) * 4 + lax.rem(pz + dz * turn, 4)
        for dx, dz in [(2, 2), (1, 2), (2, 1), (3, 2), (2, 3), (1, 1), (3, 3), (1, 3), (3, 1), (2, 0), (0, 2), (1, 0), (0, 1), (3, 0), (0, 3)]
    ]

    def rows_of(r):
        return pl.ds(pl.multiple_of(r * LANES, LANES), LANES)

    load_store = pltpu.make_async_copy(store_hbm, mix, in_sems.at[0])
    load_pair = pltpu.make_async_copy(pair_hbm, pair_in, in_sems.at[1])
    loads = [
        pltpu.make_async_copy(source, target, in_sems.at[2 + n])
        for n, (source, target) in enumerate(
            ((q_hbm, q_in), (k_hbm, k_in), (v_hbm, v_in), (gate_hbm, gate_in))
        )
    ]
    load_store.start()

    def load_query(e, carry):
        r, h = e // 8, lax.rem(e, 8)
        pltpu.make_async_copy(
            soft_q_hbm.at[rows_of(r), rows_of(h)], q_cat.at[r, rows_of(h)], in_sems.at[6]
        ).start()
        return carry

    page_start = lax.broadcasted_iota(jnp.int32, (1, 32), 1) * LANES
    wants[...] = jnp.full((8, LANES), 4095, jnp.int32)
    for r in range(4):
        ids = page_holder[r : r + 1, :] * 16 + page_local[r : r + 1, :]
        wants[0:1, r * 32 : r * 32 + 32] = jnp.where(page_start < lengths[r], ids, 4095)
        wants[1:2, r * 8 : r * 8 + 8] = state_slot[r : r + 1, :]

    barrier = pltpu.get_barrier_semaphore()
    for d in heads_to:
        pl.semaphore_signal(barrier, inc=1, device_id={"head": d}, device_id_type=MESH)
    for d in pools_to:
        pl.semaphore_signal(barrier, inc=1, device_id={"pool": d}, device_id_type=MESH)
    pl.semaphore_wait(barrier, 22)

    for d in pools_to:
        pltpu.make_async_remote_copy(
            wants,
            asked.at[pool],
            ask_sems.at[0],
            ask_sems.at[1],
            device_id={"pool": d},
            device_id_type=MESH,
        ).start()
    asked[pool] = wants[...]

    def send_store(t, carry):
        part = pl.ds(pl.multiple_of(t * tokens, tokens), tokens)
        for d in heads_to:
            pltpu.make_async_remote_copy(
                kv_ref.at[:, d, part, :],
                a_buf.at[t, pl.ds(head * 16, 16)],
                a_send.at[t],
                a_recv.at[t],
                device_id={"head": d},
                device_id_type=MESH,
            ).start()
        pltpu.make_async_copy(
            kv_ref.at[:, head, part, :], a_buf.at[t, pl.ds(head * 16, 16)], a_recv.at[t]
        ).start()
        return carry

    lax.fori_loop(0, 2, send_store, 0)

    load_pair.start()
    lax.fori_loop(0, 32, load_query, 0)
    for load in loads:
        load.start()
    wait_bytes(asked.at[pl.ds(0, 15)], ask_sems.at[1])
    state_lists(pool, wants, asked, st_lists)
    to_scalars = pltpu.make_async_copy(st_lists, st_table, list_sems.at[0])
    to_scalars.start()
    to_scalars.wait()

    load_store.wait()

    def pack_state(i, carry):
        for c in range(STATE_CAP):
            st_send[i * STATE_CAP + c] = mix[st_table[i, c]].astype(bf16)
        return carry

    lax.fori_loop(0, 16, pack_state, 0)
    mine_st = pl.ds(pool * STATE_CAP, STATE_CAP)
    for first in range(0, STATE_CAP, STATE_PIECE):
        for d in pools_to:
            pltpu.make_async_remote_copy(
                st_send.at[pl.ds(d * STATE_CAP + first, STATE_PIECE)],
                st_recv.at[pl.ds(pool * STATE_CAP + first, STATE_PIECE)],
                st_sems.at[0],
                st_sems.at[1],
                device_id={"pool": d},
                device_id_type=MESH,
            ).start()
    pltpu.make_async_copy(st_send.at[mine_st], st_recv.at[mine_st], st_sems.at[1]).start()

    page_lists(row_cap, pool, wants, asked, lists)
    to_table = pltpu.make_async_copy(lists, table, list_sems.at[1])
    to_table.start()
    lax.fori_loop(2, CHUNKS, send_store, 0)
    to_table.wait()
    crowd_out[0, 0] = table[49, 0]

    temper = LOG2E / math.sqrt(LANES)
    row_i = lax.broadcasted_iota(jnp.int32, (LANES, LANES), 0)
    col_i = lax.broadcasted_iota(jnp.int32, (LANES, LANES), 1)

    def open_softmax(e, carry):
        r, h = e // 8, lax.rem(e, 8)
        q = q_cat[r, rows_of(h), :]
        k = pair_in[rows_of(r), :LANES]
        v = pair_in[rows_of(r), LANES:]
        s = lax.dot_general(q, k, (((1,), (1,)), ((), ())), preferred_element_type=f32) * temper
        s = jnp.where(col_i <= row_i, s, -1e30)
        peak = jnp.max(s, axis=1, keepdims=True)
        p = jnp.exp2(s - peak)
        acc[r, rows_of(h), :LANES] = jnp.dot(p.astype(bf16), v, preferred_element_type=f32)
        acc[r, rows_of(h), LANES:] = p
        top[r, rows_of(h), :] = jnp.broadcast_to(peak, (LANES, LANES))
        return carry


    lane = lax.broadcasted_iota(jnp.int32, (1, keys), 1)

    def attend_chunk(t):
        wait_bytes(r_buf.at[t, pl.ds(0, 15 * row_cap)], b_recv.at[t])
        wait_bytes(r_buf.at[t, pl.ds(0, 3 * EXTRA)], z_recv.at[t])
        r_cur[...] = r_buf[t]
        spot = (lane // tokens) * LANES + t * tokens + lax.rem(lane, tokens)

        def one_request(r, carry):
            for p in range(32):
                block = r_cur[table[48, r * 32 + p]]
                key_buf[p * tokens : (p + 1) * tokens, :] = block[:, :LANES]
                val_buf[p * tokens : (p + 1) * tokens, :] = block[:, LANES:]
            bias = jnp.where(spot < lengths[r], 0.0, -1e30).astype(f32)

            s = lax.dot_general(
                q_cat[r], key_buf[...], (((1,), (1,)), ((), ())), preferred_element_type=f32
            )
            s = s * temper + bias
            before = top[r]
            peak = jnp.maximum(before, jnp.max(s, axis=1, keepdims=True))
            p = jnp.exp2(s - jnp.concatenate([peak] * (keys // LANES), axis=1))
            shrink = jnp.exp2(before - peak)
            acc[r, :, :LANES] = acc[r, :, :LANES] * shrink + jnp.dot(
                p.astype(bf16), val_buf[...], preferred_element_type=f32
            )
            sums = p[:, :LANES]
            for part in range(1, keys // LANES):
                sums = sums + p[:, part * LANES : (part + 1) * LANES]
            acc[r, :, LANES:] = acc[r, :, LANES:] * shrink + sums
            top[r] = peak
            return carry

        lax.fori_loop(0, 4, one_request, 0)

    def light_request(r):
        spacing = (row_i - col_i).astype(f32)
        steps = lax.broadcasted_iota(jnp.int32, (LANES, 1), 0).astype(f32)

        def one_head(h, total):
            rate = rates[h]
            rows, cols = rows_of(r), rows_of(h)
            q, k, v = q_in[rows, cols], k_in[rows, cols], v_in[rows, cols]
            state = st_recv[st_table[16, r * 8 + h]]
            weights = jnp.where(spacing >= 0.0, jnp.exp(-rate * jnp.maximum(spacing, 0.0)), 0.0)
            s = lax.dot_general(q, k, (((1,), (1,)), ((), ())), preferred_element_type=f32) * weights
            inside = jnp.dot(s.astype(bf16), v, preferred_element_type=f32)
            carried = jnp.dot(q, state, preferred_element_type=f32) * jnp.exp(-rate * (steps + 1.0))
            out = inside + carried
            mix[r * 8 + h] = out
            trail = k.astype(f32) * jnp.exp(-rate * (LANES - 1.0 - steps))
            high = trail.astype(bf16)
            low = (trail - high.astype(f32)).astype(bf16)
            across = (((0,), (0,)), ((), ()))
            state_out[r * 8 + h] = (
                state.astype(f32) * jnp.exp(jnp.full((1, 1), -LANES, f32) * rate)
                + lax.dot_general(high, v, across, preferred_element_type=f32)
                + lax.dot_general(low, v, across, preferred_element_type=f32)
            )
            return total + jnp.sum(out * out, axis=1, keepdims=True)

        total = lax.fori_loop(0, 8, one_head, jnp.zeros((LANES, 1), f32))
        sq_send[r] = jnp.broadcast_to(total, (LANES, LANES)).T[:8, :]

    def send_chunk(t):
        wait_bytes(a_buf.at[t], a_recv.at[t])
        slot = lax.rem(t, SLOTS)

        @pl.when(t >= SLOTS)
        def _():
            wait_bytes(s_buf.at[slot, pl.ds(0, 15 * row_cap)], b_send.at[slot])

        a_cur[...] = a_buf[t]

        def along_x(x, e):
            spot = table[16 + 4 * x, e]
            for z in range(1, 4):
                spot = spot + table[16 + 4 * x + z, e]
            return a_cur[spot]

        for e in range(EXTRA):
            for x in range(4):
                xs_buf[t, x * EXTRA + e] = along_x(x, e)
            xo_buf[t, px * EXTRA + e] = along_x(px, e)
        for x in xs_to:
            pltpu.make_async_remote_copy(
                xs_buf.at[t, pl.ds(x * EXTRA, EXTRA)],
                xo_buf.at[t, pl.ds(px * EXTRA, EXTRA)],
                x_send.at[t],
                x_recv.at[t],
                device_id={"pool": x * 4 + pz},
                device_id_type=MESH,
            ).start()

        def pack(i, inner):
            for c in range(row_cap):
                s_buf[slot, i * row_cap + c] = a_cur[table[i, c]]
            return inner

        lax.fori_loop(0, 16, pack, 0)
        for first in range(0, row_cap, PIECE):
            size = min(PIECE, row_cap - first)
            for d in pools_to:
                pltpu.make_async_remote_copy(
                    s_buf.at[slot, pl.ds(d * row_cap + first, size)],
                    r_buf.at[t, pl.ds(pool * row_cap + first, size)],
                    b_send.at[slot],
                    b_recv.at[t],
                    device_id={"pool": d},
                    device_id_type=MESH,
                ).start()
        for c in range(row_cap):
            r_buf[t, pool * row_cap + c] = a_cur[table[pool, c]]

    def relay_chunk(t):
        wait_bytes(xo_buf.at[t, pl.ds(0, 3 * EXTRA)], x_recv.at[t])
        xo_cur[...] = xo_buf[t]
        for e in range(EXTRA):
            for z in range(4):
                zs_buf[t, z * EXTRA + e] = xo_cur[table[32 + px * 4 + z, e]]
            r_buf[t, 16 * row_cap + pz * EXTRA + e] = xo_cur[table[32 + pool, e]]
        for z in zs_to:
            pltpu.make_async_remote_copy(
                zs_buf.at[t, pl.ds(z * EXTRA, EXTRA)],
                r_buf.at[t, pl.ds(16 * row_cap + pz * EXTRA, EXTRA)],
                z_send.at[t],
                z_recv.at[t],
                device_id={"pool": px * 4 + z},
                device_id_type=MESH,
            ).start()


    def finish_light(r, carry):
        squares = jnp.sum(sq_recv[:, r, :1, :], axis=0)
        factor = lax.rsqrt(squares / (64.0 * LANES) + 1e-06)
        column = jnp.broadcast_to(factor, (LANES, LANES)).T[:, :1]
        rows = rows_of(r)

        def one_head(h, inner):
            cols = rows_of(h)
            gate = jax.nn.sigmoid(gate_in[rows, cols].astype(f32))
            light_out[rows, cols] = (mix[r * 8 + h] * column * gain_in[:, cols] * gate).astype(bf16)
            return inner

        return lax.fori_loop(0, 8, one_head, carry)

    save_light = pltpu.make_async_copy(light_out, light_hbm, out_sems.at[0])
    save_state = pltpu.make_async_copy(state_out, state_hbm, out_sems.at[1])

    def step(t, carry):
        @pl.when(t < CHUNKS)
        def _():
            send_chunk(t)

        @pl.when(t == 0)
        def _():
            load_pair.wait()
            wait_bytes(q_cat, in_sems.at[6])
            lax.fori_loop(0, 32, open_softmax, 0)

        @pl.when((t >= 1) & (t <= CHUNKS))
        def _():
            relay_chunk(t - 1)

        @pl.when(t == 2)
        def _():
            wait_bytes(st_recv, st_sems.at[1])
            for load in loads:
                load.wait()

        @pl.when((t >= 2) & (t < 6))
        def _():
            light_request(t - 2)

        @pl.when(t == 6)
        def _():
            sq_recv[head] = sq_send[...]
            for d in heads_to:
                pltpu.make_async_remote_copy(
                    sq_send,
                    sq_recv.at[head],
                    sq_sems.at[0],
                    sq_sems.at[1],
                    device_id={"head": d},
                    device_id_type=MESH,
                ).start()

        @pl.when(t == CHUNKS)
        def _():
            wait_bytes(sq_recv.at[pl.ds(0, 7)], sq_sems.at[1])
            lax.fori_loop(0, 4, finish_light, 0)
            save_light.start()
            save_state.start()

        @pl.when(t >= LAG)
        def _():
            attend_chunk(t - LAG)

        return carry


    lax.fori_loop(0, CHUNKS + LAG, step, 0)

    def finish_soft(e, carry):
        r, h = e // 8, lax.rem(e, 8)
        soft_out[rows_of(r), rows_of(h)] = (
            acc[r, rows_of(h), :LANES] / jnp.sum(acc[r, rows_of(h), LANES:], axis=1, keepdims=True)
        ).astype(bf16)
        return carry

    lax.fori_loop(0, 32, finish_soft, 0)

    def drain(t, carry):
        wait_bytes(a_buf.at[t, pl.ds(0, 112)], a_send.at[t])
        wait_bytes(xs_buf.at[t, pl.ds(0, 3 * EXTRA)], x_send.at[t])
        wait_bytes(zs_buf.at[t, pl.ds(0, 3 * EXTRA)], z_send.at[t])
        return carry

    lax.fori_loop(0, CHUNKS, drain, 0)
    for slot in range(SLOTS):
        wait_bytes(s_buf.at[slot, pl.ds(0, 15 * row_cap)], b_send.at[slot])
    wait_bytes(st_send.at[pl.ds(0, 15 * STATE_CAP)], st_sems.at[0])
    wait_bytes(sq_recv.at[pl.ds(0, 7)], sq_sems.at[0])
    wait_bytes(asked.at[pl.ds(0, 15)], ask_sems.at[0])
    save_light.wait()
    save_state.wait()


def fused_call(row_cap, lengths, rates, page_holder, page_local, state_slot, gain, q, k, v, gate, store, soft_q, pair, kv):
    tokens = LANES // CHUNKS
    bf16, f32 = jnp.bfloat16, jnp.float32
    vmem, smem = pl.BlockSpec(memory_space=pltpu.VMEM), pl.BlockSpec(memory_space=pltpu.SMEM)
    hbm = pl.BlockSpec(memory_space=pl.ANY)
    dma = pltpu.SemaphoreType.DMA
    return pl.pallas_call(
        functools.partial(fused_kernel, row_cap),
        out_shape=(
            jax.ShapeDtypeStruct((512, 1024), bf16),
            jax.ShapeDtypeStruct((32, LANES, LANES), f32),
            jax.ShapeDtypeStruct((512, 1024), bf16),
            jax.ShapeDtypeStruct((1, 1), jnp.int32),
        ),
        in_specs=[smem, smem, vmem, vmem, vmem, vmem] + [hbm] * 8,
        out_specs=(hbm, hbm, vmem, smem),
        scratch_shapes=[
            pltpu.VMEM((512, 1024), bf16),
            pltpu.VMEM((512, 1024), bf16),
            pltpu.VMEM((512, 1024), bf16),
            pltpu.VMEM((512, 1024), bf16),
            pltpu.VMEM((512, 256), bf16),
            pltpu.VMEM((512, 1024), bf16),
            pltpu.VMEM((32, LANES, LANES), f32),
            pltpu.VMEM((CHUNKS, 128, tokens, 256), bf16),
            pltpu.VMEM((128, tokens, 256), bf16),
            pltpu.VMEM((SLOTS, 16 * row_cap, tokens, 256), bf16),
            pltpu.VMEM((CHUNKS, 16 * row_cap + 4 * EXTRA, tokens, 256), bf16),
            pltpu.VMEM((16 * row_cap + 4 * EXTRA, tokens, 256), bf16),
            pltpu.VMEM((32 * tokens, LANES), bf16),
            pltpu.VMEM((32 * tokens, LANES), bf16),
            pltpu.VMEM((16 * STATE_CAP, LANES, LANES), bf16),
            pltpu.VMEM((16 * STATE_CAP, LANES, LANES), bf16),
            pltpu.VMEM((32, LANES, LANES), f32),
            pltpu.VMEM((4, 8, LANES), f32),
            pltpu.VMEM((8, 4, 8, LANES), f32),
            pltpu.VMEM((4, 1024, LANES), bf16),
            pltpu.VMEM((4, 1024, 2 * LANES), f32),
            pltpu.VMEM((4, 1024, LANES), f32),
            dma((CHUNKS,)),
            dma((CHUNKS,)),
            dma((SLOTS,)),
            dma((CHUNKS,)),
            pltpu.VMEM((CHUNKS, 4 * EXTRA, tokens, 256), bf16),
            pltpu.VMEM((CHUNKS, 4 * EXTRA, tokens, 256), bf16),
            pltpu.VMEM((4 * EXTRA, tokens, 256), bf16),
            pltpu.VMEM((CHUNKS, 4 * EXTRA, tokens, 256), bf16),
            dma((CHUNKS,)),
            dma((CHUNKS,)),
            dma((CHUNKS,)),
            dma((CHUNKS,)),
            dma((2,)),
            dma((2,)),
            pltpu.VMEM((8, LANES), jnp.int32),
            pltpu.VMEM((16, 8, LANES), jnp.int32),
            pltpu.VMEM((24, LANES), jnp.int32),
            pltpu.SMEM((24, LANES), jnp.int32),
            pltpu.VMEM((56, LANES), jnp.int32),
            pltpu.SMEM((56, LANES), jnp.int32),
            dma((2,)),
            dma((2,)),
            dma((7,)),
            dma((2,)),
        ],
        compiler_params=pltpu.CompilerParams(
            collective_id=1, has_side_effects=True, vmem_limit_bytes=63 * 2**20
        ),
        cost_estimate=pl.CostEstimate(flops=10**10, bytes_accessed=3 * 10**7, transcendentals=2 * 10**7),
    )(lengths, rates, page_holder, page_local, state_slot, gain, q, k, v, gate, store, soft_q, pair, kv)


def keep_kernel(*refs):
    half = len(refs) // 2
    for n in range(half):
        refs[half + n][...] = refs[n][...]


def keep_results(*arrays):
    steps = 8
    specs = [
        pl.BlockSpec(
            (x.shape[0] // steps,) + x.shape[1:], lambda i, rank=x.ndim: (i,) + (0,) * (rank - 1)
        )
        for x in arrays
    ]
    return pl.pallas_call(
        keep_kernel,
        grid=(steps,),
        out_shape=tuple(jax.ShapeDtypeStruct(x.shape, x.dtype) for x in arrays),
        in_specs=specs,
        out_specs=tuple(specs),
        compiler_params=pltpu.CompilerParams(vmem_limit_bytes=16 * 2**20),
    )(*arrays)


def body(
    light_query,
    light_key,
    light_value,
    light_gate,
    decay_rate,
    norm_gain,
    state_store,
    state_slot,
    soft_query,
    soft_pair,
    kv_store,
    page_holder,
    page_local,
    prefix_len,
):
    light, states, soft, crowd = fused_call(
        ROW_CAP,
        prefix_len,
        decay_rate,
        page_holder.reshape(4, 32),
        page_local,
        state_slot,
        norm_gain.reshape(1, -1),
        light_query,
        light_key,
        light_value,
        light_gate,
        state_store.reshape(32, LANES, LANES),
        soft_query,
        soft_pair,
        kv_store,
    )

    def quick():
        kept = keep_results(light, states, soft)
        return kept[0], kept[1].reshape(4, 8, LANES, LANES), kept[2]

    def general():
        return general_body(
            light_query,
            light_key,
            light_value,
            light_gate,
            decay_rate,
            norm_gain,
            state_store,
            state_slot,
            soft_query,
            soft_pair,
            kv_store,
            page_holder,
            page_local,
            prefix_len,
        )

    return lax.cond(crowd[0, 0] <= EXTRA, quick, general)


def solution(mesh):
    return jax.shard_map(
        body,
        mesh=mesh,
        in_specs=(
            P("pool", "head"),
            P("pool", "head"),
            P("pool", "head"),
            P("pool", "head"),
            P("head"),
            P("head"),
            P("pool", "head", None, None),
            P("pool", "head"),
            P("pool", "head"),
            P("pool", "head"),
            P(("pool", "head"), None, None, None),
            P("pool", None, None),
            P("pool", None),
            P("pool"),
        ),
        out_specs=(P("pool", "head"), P("pool", "head", None, None), P("pool", "head")),
        check_vma=False,
    )
```
